32 devices in a mesh: shot: 8 (over y, x, core), freq: 4 (over z).
Axes of the slice: x: 2, y: 2, z: 4, core: 2. Of those that a mesh axis runs over, the one named last changes fastest.
Arguments:
- traces: float32 [32, 2048, 1024], P('shot', 'freq'), may hold values from -6 to 6
- interp_weights: float32 [32, 16, 128, 128], P('shot'), may hold values from -0.09375 to 0.09375
- tile_ids: int32 [32, 16], P('shot'), may hold values from 0 to 15, as said below
Outputs:
- binned: float32 [16, 2, 384, 128], P('shot', None, 'freq')
The draws below stay inside these ranges and needn't reach their ends.
Inputs may be any that keep to these rules, and one draw needn't show every extreme that they name: `tile_ids`: tile g is owned by index g // 2 of shot. Among the receiver blocks of the shots of one index of shot, at most 10 land on tiles of one owner, and in every draw each index of shot sends exactly 10 to one owner.
All inputs are finite; a program needn't handle non-finite values.
Results may differ from the reference program's by a relative error of at most 0.0003.
Values sent between devices are 32-bit elements; how exact they have to be, the bound alone decides.
No kernel may reach another device: no remote copies, remote signals or barrier semaphores. Data moves between devices by JAX's collectives and lax.ppermute only.
A program may use at most 128 MiB of HBM per device.

```python
import math
import jax
import jax.numpy as jnp
from jax import lax

SH_DEV = 4
RECS = 2048
NT = 1024
NF = 384
RB = 128
TILE = 128
TILES_DEV = 2
SHOTS = 32
NRB = 16
NTILES = 16
CAP = 10


def draw_tile_ids(key, part):
    owners = NTILES // TILES_DEV
    row_count = SH_DEV * NRB
    block_count = SHOTS // SH_DEV

    def one_block(block_key):
        key_hot, key_shift, key_perm, key_sub = jax.random.split(block_key, 4)
        hottest = jax.random.randint(key_hot, (), 0, owners)
        offset = jax.random.randint(key_shift, (), 0, owners - 1)
        position = jnp.arange(row_count, dtype=jnp.int32)
        others = (hottest + 1 + (position - CAP + offset) % (owners - 1)) % owners
        target = jnp.where(position < CAP, hottest, others)
        order = jax.random.permutation(key_perm, row_count)
        target = target[order]
        within = jax.random.randint(key_sub, (row_count,), 0, TILES_DEV)
        return (target * TILES_DEV + within).astype(jnp.int32)
    block_keys = jax.random.split(jax.random.fold_in(key, 7), block_count)
    return jax.vmap(one_block)(block_keys).reshape(SHOTS, NRB)


def level_of(key, dims, shards, smallest, top_value):
    level = 1.0
    for dim, blocks in shards:
        steps = jax.random.uniform(jax.random.fold_in(jax.random.fold_in(key, 6), dim), (blocks,), jnp.float32, smallest / len(shards), top_value / len(shards))
        level = level * jnp.repeat(jnp.exp(steps), dims[dim] // blocks).reshape((-1,) + (1,) * (len(dims) - 1 - dim))
    return level


def bell_draw(key, dims, width, bound, cuts=(), kind=jnp.bfloat16):
    level = level_of(key, dims, cuts, -0.22, 0.18) if cuts else 1.0
    result = jax.random.normal(key, dims, jnp.float32) * width * level
    return jnp.minimum(jnp.maximum(result, -bound), bound).astype(kind)


def setup_inputs(seed: int = 0) -> dict:
    arg_keys = jax.random.split(jax.random.key(seed), 4)
    traces = bell_draw(arg_keys[0], (SHOTS, RECS, NT), 1.0, 6.0, ((0, 8), (1, 4)), jnp.float32)
    interp_weights = bell_draw(arg_keys[1], (SHOTS, NRB, RB, TILE), (RB * SH_DEV * NRB // TILES_DEV) ** -0.5, 0.09375, ((0, 8),), jnp.float32)
    tile_ids = draw_tile_ids(jax.random.fold_in(arg_keys[3], 71), 0)
    return dict(traces=traces, interp_weights=interp_weights, tile_ids=tile_ids)


def reference(traces, interp_weights, tile_ids):

    def one_shot(binned, shot_data):
        gather_t, weights, tile_row = shot_data
        spec = jnp.fft.rfft(gather_t, axis=-1)[:, :NF] / math.sqrt(NT)
        parts = jnp.stack([jnp.real(spec), jnp.imag(spec)])
        parts = jnp.transpose(parts, (0, 2, 1)).reshape(2 * NF, NRB, RB)
        partial_value = jnp.einsum('cbr,brt->bct', parts, weights, precision=lax.Precision.HIGHEST)
        onehot = (tile_row[None, :] == jnp.arange(NTILES, dtype=jnp.int32)[:, None]).astype(partial_value.dtype)
        added = jnp.dot(onehot, partial_value.reshape(NRB, 2 * NF * TILE), precision=lax.Precision.HIGHEST)
        return (binned + added, None)
    start = jnp.zeros((NTILES, 2 * NF * TILE), jnp.float32)
    binned, unused = lax.scan(one_shot, start, (traces, interp_weights, tile_ids))
    return binned.reshape(NTILES, 2, NF, TILE)
```

```python
import math

import jax
import jax.numpy as jnp
import numpy as np
from jax import lax
from jax.experimental import pallas as pl
from jax.experimental.pallas import tpu as pltpu
from jax.sharding import PartitionSpec as P

NF = 384
TILES_DEV = 2
RADIX = 4
GROUPS = ((0, 2), (1, 3))
PAIR = 2


def bit_orders(shot_count):
    bits = list(range(1, shot_count.bit_length() - 1))
    turn = len(bits) // 2
    return bits, bits[turn:] + bits[:turn]


def dft_table(residues, freq_count, time_len):
    fold = time_len // RADIX
    freq_here = NF // freq_count
    rows = []
    for owner in range(freq_count):
        for residue in residues:
            freqs = owner * freq_here + np.arange(residue, freq_here, RADIX)
            angle = 2.0 * math.pi / time_len * (freqs[:, None] * np.arange(fold)[None, :] % time_len)
            cos, sin = np.cos(angle), np.sin(angle)
            if residue % 2 == 0:
                rows += [cos, -sin]
            else:
                sign = 1.0 if residue == 1 else -1.0
                rows += [np.hstack([cos, -sign * sin]), np.hstack([-sin, -sign * cos])]
    table = np.concatenate(rows) / math.sqrt(time_len)
    return table.reshape(freq_count, -1, table.shape[-1]).astype(np.float32)


def split(value):
    high = value.astype(jnp.bfloat16)
    return high, (value - high.astype(jnp.float32)).astype(jnp.bfloat16)


def dot_nt(a, b):
    return lax.dot_general(a, b, (((1,), (1,)), ((), ())), preferred_element_type=jnp.float32)


def bin_kernel(residues, freq_count, half, meta, x_ref, w_ref, t_ref, far_ref, own_ref, table):
    step = pl.program_id(0)
    slot_count = pl.num_programs(0) * PAIR
    fold = x_ref.shape[-1] // RADIX
    even = residues[0] % 2 == 0
    per_owner = t_ref.shape[1]

    @pl.when(step == 0)
    def _():
        far_ref[...] = jnp.zeros_like(far_ref)
        own_ref[...] = jnp.zeros_like(own_ref)
        me = meta[slot_count]
        parts = [t_ref[jnp.bitwise_xor(me, i)] for i in range(freq_count)]
        if even:
            sub = per_owner // len(residues)
            parts = [part[r * sub : (r + 1) * sub] for r in range(len(residues)) for part in parts]
        high, low = split(jnp.concatenate(parts, axis=0))
        table[...] = jnp.concatenate([high, low, high], axis=1)

    x = x_ref[0]
    x0, x1, x2, x3 = (x[:, i * fold : (i + 1) * fold] for i in range(RADIX))
    if even:
        plus, cross = x0 + x2, x1 + x3
        rows = freq_count * per_owner // len(residues)
        sub = per_owner // len(residues)
        spectra = []
        for r, folded in enumerate((plus + cross, plus - cross)):
            high, low = split(folded)
            spectra.append(dot_nt(table[r * rows : (r + 1) * rows, :], jnp.concatenate([high, high, low], axis=1)))
        spectrum = jnp.concatenate(
            [s[i * sub : (i + 1) * sub] for i in range(freq_count) for s in spectra], axis=0
        )
    else:
        high, low = split(jnp.concatenate([x0 - x2, x1 - x3], axis=1))
        spectrum = dot_nt(table[...], jnp.concatenate([high, high, low], axis=1))
    block = w_ref.shape[2]
    for h in range(PAIR):
        s_high, s_low = split(spectrum[:, h * block : (h + 1) * block])
        w_high, w_low = split(w_ref[0, h])
        weights = jnp.concatenate(
            [
                jnp.concatenate([w_high, w_low], axis=1),
                jnp.concatenate([w_high, jnp.zeros_like(w_low)], axis=1),
            ],
            axis=0,
        )
        both = jnp.dot(
            jnp.concatenate([s_high, s_low], axis=1), weights, preferred_element_type=jnp.float32
        )
        tile_len = both.shape[1] // 2
        value = both[:, :tile_len] + both[:, tile_len:]
        slot = meta[step * PAIR + h]

        @pl.when(slot >= half)
        def _():
            far_ref[slot - half] += value

        @pl.when(slot < half)
        def _():
            own_ref[slot] += value


def bin_group(meta, traces, interp_weights, residues, freq_count, half):
    shots_here, recs_here, time_len = traces.shape
    block_len, tile_len = interp_weights.shape[2:]
    blocks_here = recs_here // block_len
    pairs = blocks_here // PAIR
    table = dft_table(residues, freq_count, time_len)
    rows = table.shape[0] * table.shape[1]
    slot_count = shots_here * blocks_here
    out = jax.ShapeDtypeStruct((half, rows, tile_len), jnp.float32)
    out_spec = pl.BlockSpec((half, rows, tile_len), lambda i, m: (0, 0, 0))

    def body(meta, *refs):
        bin_kernel(residues, freq_count, half, meta, *refs)

    return pl.pallas_call(
        body,
        grid_spec=pltpu.PrefetchScalarGridSpec(
            num_scalar_prefetch=1,
            grid=(shots_here * pairs,),
            in_specs=[
                pl.BlockSpec((1, PAIR * block_len, time_len), lambda i, m: (i // pairs, i % pairs, 0)),
                pl.BlockSpec(
                    (1, PAIR, block_len, tile_len),
                    lambda i, m: (i // pairs, m[slot_count] * pairs + i % pairs, 0, 0),
                ),
                pl.BlockSpec(table.shape, lambda i, m: (0, 0, 0)),
            ],
            out_specs=[out_spec, out_spec],
            scratch_shapes=[pltpu.VMEM((rows, 3 * table.shape[-1]) if residues[0] % 2 else (rows, 3 * table.shape[-1]), jnp.bfloat16)],
        ),
        out_shape=[out, out],
        compiler_params=pltpu.CompilerParams(vmem_limit_bytes=56 << 20),
        cost_estimate=pl.CostEstimate(
            flops=2 * 3 * rows * table.shape[-1] * block_len * slot_count,
            bytes_accessed=traces.size * 4 + 2 * half * rows * tile_len * 4,
            transcendentals=0,
        ),
        name="bin_group",
    )(meta, traces, interp_weights, table)


def shards(traces, interp_weights, tile_ids):
    shot_count = lax.axis_size("shot")
    freq_count = lax.axis_size("freq")
    shots_here, recs_here, time_len = traces.shape
    block_len, tile_len = interp_weights.shape[2:]
    blocks_here = recs_here // block_len
    half = shot_count // 2 * TILES_DEV
    me_shot = lax.axis_index("shot")
    me_freq = lax.axis_index("freq")
    orders = bit_orders(shot_count)

    tiles = lax.dynamic_slice_in_dim(tile_ids, me_freq * blocks_here, blocks_here, axis=1).reshape(-1)
    owner = tiles // TILES_DEV
    apart = owner ^ me_shot

    def place(order):
        index = jnp.zeros_like(apart)
        for bit in order:
            index = index * 2 + ((apart >> bit) & 1)
        return index

    index = jnp.where(owner & 1 == 0, place(orders[0]), place(orders[1]))
    slots = (apart & 1) * half + index * TILES_DEV + tiles % TILES_DEV
    meta = jnp.concatenate([slots, me_freq[None]]).astype(jnp.int32)

    def shot_pairs(flip):
        return [(i, i ^ flip(i & 1)) for i in range(shot_count)]

    def freq_pairs(flip):
        return [(i, i ^ flip) for i in range(freq_count)]

    groups = []
    for residues in GROUPS:
        far, own = bin_group(meta, traces, interp_weights, residues, freq_count, half)
        groups.append((far, own))
    results = []
    for residues, (far, own) in zip(GROUPS, groups):
        value = own + lax.ppermute(far, "shot", shot_pairs(lambda core: 1))
        for level in range(len(orders[0])):
            keep = value.shape[0] // 2
            got = lax.ppermute(value[keep:], "shot", shot_pairs(lambda core: 1 << orders[core][level]))
            value = value[:keep] + got
        value = value.reshape(TILES_DEV, freq_count, -1, tile_len)
        flip = 1
        while flip < freq_count:
            value = value.reshape(TILES_DEV, -1, 2, value.shape[-2], tile_len)
            got = lax.ppermute(value[:, :, 1], "freq", freq_pairs(flip))
            value = value[:, :, 0] + got
            flip *= 2
        results.append(value.reshape(TILES_DEV, len(residues), 2, -1, tile_len))
    both = jnp.stack(results, axis=2)
    both = both.reshape(TILES_DEV, RADIX, 2, -1, tile_len)
    return both.transpose(0, 2, 3, 1, 4).reshape(TILES_DEV, 2, NF // freq_count, tile_len)


def solution(mesh):
    in_specs = (P("shot", "freq", None), P("shot", None, None, None), P("shot", None))
    out_specs = P("shot", None, "freq", None)
    return jax.shard_map(shards, mesh=mesh, in_specs=in_specs, out_specs=out_specs, check_vma=False)
```

```python
import math

import jax
import jax.numpy as jnp
import numpy as np
from jax import lax
from jax.experimental import pallas as pl
from jax.experimental.pallas import tpu as pltpu
from jax.sharding import PartitionSpec as P

NF = 384
TILES_DEV = 2
GROUPS = ((0, 4), (2, 6), (1, 7), (3, 5))
CHUNKS = ((0, 1), (2, 3))
ORDERS = ("csz", "csz")
CALLS = ((0,), (1,))
DEPTH = 2
VMEM_SUMS = 16 << 20
VMEM_LIMIT = 24 << 20


def bit_orders(shot_count):
    bits = list(range(1, shot_count.bit_length() - 1))
    turn = len(bits) // 2
    return bits, bits[turn:] + bits[:turn]


def dft_tables(groups, freq_count, time_len):
    freq_here = NF // freq_count
    scale = 1.0 / math.sqrt(time_len)
    tables = []
    for g in groups:
        residues = GROUPS[g]
        rows = []
        for owner in range(freq_count):
            if residues[0] % 2 == 0:
                freqs = owner * freq_here + np.arange(residues[0], freq_here, 4)
                angle = 2.0 * math.pi / time_len * (freqs[:, None] * np.arange(time_len // 4) % time_len)
                rows += [np.cos(angle), -np.sin(angle)]
            else:
                for residue in residues:
                    freqs = owner * freq_here + np.arange(residue, freq_here, 8)
                    angle = 2.0 * math.pi / time_len * (freqs[:, None] * np.arange(time_len // 8) % time_len)
                    cos, sin = np.cos(angle), np.sin(angle)
                    sign = 1.0 if residue in (1, 5) else -1.0
                    rows += [np.hstack([cos, -sign * sin]), np.hstack([-sin, -sign * cos])]
        tables.append((np.concatenate(rows) * scale).reshape(freq_count, -1, time_len // 4))
    return np.stack(tables).astype(np.float32)


def fold(x, groups):
    eighth = x.shape[1] // 8
    q0, q1, q2, q3 = (x[:, 2 * i * eighth : 2 * (i + 1) * eighth] for i in range(4))
    folded = {}
    if 0 in groups or 1 in groups:
        plus, cross = q0 + q2, q1 + q3
        folded[0], folded[1] = plus + cross, plus - cross
    if 2 in groups or 3 in groups:
        d02, d13 = q0 - q2, q1 - q3
        d0, d1, d2, d3 = d02[:, :eighth], d02[:, eighth:], d13[:, :eighth], d13[:, eighth:]
        root = math.sqrt(0.5)
        near, far = (d1 - d3) * root, (d1 + d3) * root
        folded[2] = jnp.concatenate([d0 + near, d2 + far], axis=1)
        folded[3] = jnp.concatenate([d0 - near, d2 - far], axis=1)
    return [folded[g] for g in groups]


def split(value):
    high = value.astype(jnp.bfloat16)
    return high, (value - high.astype(jnp.float32)).astype(jnp.bfloat16)


def dot_nt(a, b):
    return lax.dot_general(a, b, (((1,), (1,)), ((), ())), preferred_element_type=jnp.float32)


def slot_of(tile, me_shot, shot_count):
    owner = tile // TILES_DEV
    apart = jnp.bitwise_xor(owner, me_shot)

    def place(order):
        index = 0
        for bit in order:
            index = index * 2 + jnp.bitwise_and(jnp.right_shift(apart, bit), 1)
        return index

    first, second = bit_orders(shot_count)
    index = jnp.where(jnp.bitwise_and(owner, 1) == 0, place(first), place(second))
    half = shot_count // 2 * TILES_DEV
    return jnp.bitwise_and(apart, 1) * half + index * TILES_DEV + jnp.bitwise_and(tile, TILES_DEV - 1)


def bin_kernel(chunks, shot_count, freq_count, load, tiles, x_ref, w_ref, t_hbm, *refs):
    outs, refs = refs[: len(chunks)], refs[len(chunks) :]
    if load:
        x_hbm, w_hbm, xbuf, wbuf = x_ref, w_ref, refs[0], refs[1]
        refs = refs[2:]
    else:
        xbuf, wbuf = x_ref, w_ref
    tbuf, table, spectra, xsem, wsem, tsem = refs
    shots_here, blocks_here, block_len, tile_len = wbuf.shape
    me_shot, me_freq = lax.axis_index("shot"), lax.axis_index("freq")
    rows = t_hbm.shape[2]
    groups = [g for chunk in chunks for g in chunk]
    place, stride, start = {}, {}, 0
    for chunk in chunks:
        for j, g in enumerate(chunk):
            place[g], stride[g] = start + j * rows, len(chunk) * rows
        start += len(chunk) * freq_count * rows

    def x_copy(i):
        return pltpu.make_async_copy(x_hbm.at[i], xbuf.at[i], xsem.at[i])

    def w_copy(i):
        return pltpu.make_async_copy(w_hbm.at[i, pl.ds(me_freq * blocks_here, blocks_here)], wbuf.at[i], wsem.at[i])

    def t_copy(i):
        return pltpu.make_async_copy(t_hbm.at[:, jnp.bitwise_xor(me_freq, i)], tbuf.at[:, i], tsem.at[i])

    for i in range(freq_count):
        t_copy(i).start()
    if load:
        x_copy(0).start()
        w_copy(0).start()
        for i in range(1, DEPTH):
            x_copy(i).start()
    for out in outs:
        out[...] = jnp.zeros_like(out)
    for i in range(freq_count):
        t_copy(i).wait()
    for n in range(len(groups)):
        high, low = split(jnp.concatenate([tbuf[n, i] for i in range(freq_count)], axis=0))
        table[n] = jnp.concatenate([high, low], axis=0)

    def transform(i, n, part):
        high, low = split(part)
        wide = dot_nt(table[n], high)
        half = wide.shape[0] // 2
        result = wide[:half] + wide[half:] + dot_nt(table[n, :half], low)
        g = groups[n]
        for j in range(freq_count):
            start = place[g] + j * stride[g]
            spectra[i % 2, start : start + rows] = result[j * rows : (j + 1) * rows]

    def spread(i, b):
        if load and b == 0:
            w_copy(i).wait()
        s_high, s_low = split(spectra[i % 2, :, b * block_len : (b + 1) * block_len])
        w_high, w_low = split(wbuf[i, b])
        weights = jnp.concatenate(
            [
                jnp.concatenate([w_high, w_low], axis=1),
                jnp.concatenate([w_high, jnp.zeros_like(w_low)], axis=1),
            ],
            axis=0,
        )
        both = jnp.dot(jnp.concatenate([s_high, s_low], axis=1), weights, preferred_element_type=jnp.float32)
        value = both[:, :tile_len] + both[:, tile_len:]
        slot = slot_of(tiles[i, me_freq * blocks_here + b], me_shot, shot_count)
        start = 0
        for out in outs:
            out[slot] += value[start : start + out.shape[1]]
            start += out.shape[1]

    for i in range(shots_here + 1):
        folded = ()
        if i < shots_here:
            if load:
                x_copy(i).wait()
                if i + DEPTH < shots_here:
                    x_copy(i + DEPTH).start()
                if i + 1 < shots_here:
                    w_copy(i + 1).start()
            folded = fold(xbuf[i], groups)
        for k in range(max(len(folded), blocks_here)):
            if k < len(folded):
                transform(i, k, folded[k])
            if i and k < blocks_here:
                spread(i - 1, k)


def bin_blocks(tile_ids, traces, interp_weights, chunks, shot_count, freq_count, load, keep):
    shots_here, recs_here, time_len = traces.shape
    block_len, tile_len = interp_weights.shape[2:]
    blocks_here = recs_here // block_len
    groups = [g for chunk in chunks for g in chunk]
    tables = jnp.asarray(dft_tables(groups, freq_count, time_len))
    rows = freq_count * tables.shape[2]
    slot_count = shot_count * TILES_DEV
    kept = [
        jax.ShapeDtypeStruct(traces.shape, jnp.float32),
        jax.ShapeDtypeStruct((shots_here, blocks_here, block_len, tile_len), jnp.float32),
    ]
    total = slot_count * len(GROUPS) * rows * tile_len * 4
    sums = pltpu.VMEM if total <= VMEM_SUMS else jax.ShapeDtypeStruct
    out_shape = [sums((slot_count, rows * len(chunk), tile_len), jnp.float32) for chunk in chunks]
    scratch = [
        pltpu.VMEM(tables.shape, jnp.float32),
        pltpu.VMEM((len(groups), 2 * rows, tables.shape[3]), jnp.bfloat16),
        pltpu.VMEM((2, len(groups) * rows, recs_here), jnp.float32),
        pltpu.SemaphoreType.DMA((shots_here,)),
        pltpu.SemaphoreType.DMA((shots_here,)),
        pltpu.SemaphoreType.DMA((freq_count,)),
    ]
    if load and keep:
        out_shape += [pltpu.VMEM(k.shape, k.dtype) for k in kept]
    elif load:
        scratch = [pltpu.VMEM(k.shape, k.dtype) for k in kept] + scratch
    place = pltpu.HBM if load else pltpu.VMEM

    def body(*refs):
        bin_kernel(chunks, shot_count, freq_count, load, *refs)

    traces = pltpu.with_memory_space_constraint(traces, place)
    interp_weights = pltpu.with_memory_space_constraint(interp_weights, place)
    tables = pltpu.with_memory_space_constraint(tables, pltpu.HBM)
    return pl.pallas_call(
        body,
        in_specs=[
            pl.BlockSpec(memory_space=pltpu.SMEM),
            pl.BlockSpec(memory_space=place),
            pl.BlockSpec(memory_space=place),
            pl.BlockSpec(memory_space=pltpu.HBM),
        ],
        out_specs=[pl.BlockSpec(memory_space=pltpu.VMEM)] * len(out_shape),
        out_shape=out_shape,
        scratch_shapes=scratch,
        compiler_params=pltpu.CompilerParams(vmem_limit_bytes=VMEM_LIMIT),
        name="bin_blocks",
    )(tile_ids, traces, interp_weights, tables)


def shards(traces, interp_weights, tile_ids):
    shot_count = lax.axis_size("shot")
    freq_count = lax.axis_size("freq")
    tile_len = interp_weights.shape[3]
    levels = bit_orders(shot_count)

    def to_core(value):
        half = value.shape[0] // 2
        got = lax.ppermute(value[half:], "shot", [(i, i ^ 1) for i in range(shot_count)])
        return value[:half] + got

    def to_shot(value, level):
        half = value.shape[0] // 2
        pairs = [(i, i ^ (1 << levels[i & 1][level])) for i in range(shot_count)]
        return value[:half] + lax.ppermute(value[half:], "shot", pairs)

    def to_freq(value, flip):
        value = value.reshape(value.shape[0], -1, 2, value.shape[2], tile_len)
        got = lax.ppermute(value[:, :, 1], "freq", [(i, i ^ flip) for i in range(freq_count)])
        return value[:, :, 0] + got

    def to_freq_direct(value):
        total = value[:, 0]
        for flip in range(freq_count - 1, 0, -1):
            total += lax.ppermute(value[:, flip], "freq", [(i, i ^ flip) for i in range(freq_count)])
        return total[:, None]

    sums = [None] * len(CHUNKS)
    for n, call in enumerate(CALLS):
        chunks = tuple(CHUNKS[c] for c in call)
        made = bin_blocks(
            tile_ids, traces, interp_weights, chunks, shot_count, freq_count, n == 0, n == 0 and len(CALLS) > 1
        )
        for c, value in zip(call, made):
            sums[c] = value
        if len(made) > len(call):
            traces, interp_weights = made[len(call) :]
    parts = [None] * len(GROUPS)
    for chunk, order, value in zip(CHUNKS, ORDERS, sums):
        value = value.reshape(value.shape[0], freq_count, -1, tile_len)
        level, flip = 0, 1
        for stage in order:
            if stage == "c":
                value = to_core(value)
            elif stage == "s":
                for level in range(len(levels[0])):
                    value = to_shot(value, level)
            elif stage == "d":
                value = to_freq_direct(value)
            else:
                flip = 1
                while flip < freq_count:
                    value = to_freq(value, flip)
                    flip *= 2
        value = value.reshape(TILES_DEV, len(chunk), -1, tile_len)
        for j, g in enumerate(chunk):
            parts[g] = value[:, j]
    eighths = {}
    for g, residues in enumerate(GROUPS):
        if residues[0] % 2 == 0:
            part = parts[g].reshape(TILES_DEV, 2, -1, 2, tile_len)
            for j, residue in enumerate(residues):
                eighths[residue] = part[:, :, :, j]
        else:
            part = parts[g].reshape(TILES_DEV, 2, 2, -1, tile_len)
            for j, residue in enumerate(residues):
                eighths[residue] = part[:, j]
    return jnp.stack([eighths[r] for r in range(8)], axis=3).reshape(TILES_DEV, 2, -1, tile_len)


def solution(mesh):
    in_specs = (P("shot", "freq", None), P("shot", None, None, None), P("shot", None))
    out_specs = P("shot", None, "freq", None)
    return jax.shard_map(shards, mesh=mesh, in_specs=in_specs, out_specs=out_specs, check_vma=False)
```

```python
import math

import jax
import jax.numpy as jnp
import numpy as np
from jax import lax
from jax.experimental import pallas as pl
from jax.experimental.pallas import tpu as pltpu
from jax.sharding import PartitionSpec as P

NF = 384
TILES_DEV = 2
GROUPS = ((0, 4), (2, 6), (1, 7), (3, 5))
CHUNKS = ((0, 1), (2, 3))
ORDERS = (("axyb", "yaxb"), ("xayb", "yaxb"))
CALLS = ((0,), (1,))
DEPTH = 2
VMEM_SUMS = 16 << 20
VMEM_LIMIT = 24 << 20


def halvings(shot_count, freq_count):
    shot_bits = [("shot", bit) for bit in range(1, shot_count.bit_length() - 1)]
    freq_bits = [("freq", bit) for bit in range(freq_count.bit_length() - 1)]
    x, a = len(shot_bits) // 2, len(freq_bits) // 2
    steps = dict(x=shot_bits[:x], y=shot_bits[x:], a=freq_bits[:a], b=freq_bits[a:])
    return [[[step for name in order for step in steps[name]] for order in orders] for orders in ORDERS]


def dft_tables(groups, freq_count, time_len):
    freq_here = NF // freq_count
    scale = 1.0 / math.sqrt(time_len)
    tables = []
    for g in groups:
        residues = GROUPS[g]
        rows = []
        for owner in range(freq_count):
            if residues[0] % 2 == 0:
                freqs = owner * freq_here + np.arange(residues[0], freq_here, 4)
                angle = 2.0 * math.pi / time_len * (freqs[:, None] * np.arange(time_len // 4) % time_len)
                rows += [np.cos(angle), -np.sin(angle)]
            else:
                for residue in residues:
                    freqs = owner * freq_here + np.arange(residue, freq_here, 8)
                    angle = 2.0 * math.pi / time_len * (freqs[:, None] * np.arange(time_len // 8) % time_len)
                    cos, sin = np.cos(angle), np.sin(angle)
                    sign = 1.0 if residue in (1, 5) else -1.0
                    rows += [np.hstack([cos, -sign * sin]), np.hstack([-sin, -sign * cos])]
        tables.append((np.concatenate(rows) * scale).reshape(freq_count, -1, time_len // 4))
    return np.stack(tables).astype(np.float32)


def fold(x, groups):
    eighth = x.shape[1] // 8
    q0, q1, q2, q3 = (x[:, 2 * i * eighth : 2 * (i + 1) * eighth] for i in range(4))
    folded = {}
    if 0 in groups or 1 in groups:
        plus, cross = q0 + q2, q1 + q3
        folded[0], folded[1] = plus + cross, plus - cross
    if 2 in groups or 3 in groups:
        d02, d13 = q0 - q2, q1 - q3
        d0, d1, d2, d3 = d02[:, :eighth], d02[:, eighth:], d13[:, :eighth], d13[:, eighth:]
        root = math.sqrt(0.5)
        near, far = (d1 - d3) * root, (d1 + d3) * root
        folded[2] = jnp.concatenate([d0 + near, d2 + far], axis=1)
        folded[3] = jnp.concatenate([d0 - near, d2 - far], axis=1)
    return [folded[g] for g in groups]


def split(value):
    high = value.astype(jnp.bfloat16)
    return high, (value - high.astype(jnp.float32)).astype(jnp.bfloat16)


def dot_nt(a, b):
    return lax.dot_general(a, b, (((1,), (1,)), ((), ())), preferred_element_type=jnp.float32)


def slots_of(tile, me_shot, steps, freq_count):
    owner = tile // TILES_DEV
    apart = jnp.bitwise_xor(owner, me_shot)
    second = jnp.bitwise_and(owner, 1) == 1
    count = len(steps[0])
    base = jnp.bitwise_and(apart, 1) << count
    for axis, bit in steps[0]:
        if axis == "shot":
            flag = jnp.bitwise_and(jnp.right_shift(apart, bit), 1)
            places = [count - 1 - order.index((axis, bit)) for order in steps]
            base += jnp.where(second, flag << places[1], flag << places[0])
    slots = []
    for far in range(freq_count):
        places = [
            sum((far >> bit & 1) << (count - 1 - i) for i, (axis, bit) in enumerate(order) if axis == "freq")
            for order in steps
        ]
        slots.append((base + jnp.where(second, places[1], places[0])) * TILES_DEV + tile % TILES_DEV)
    return slots


def bin_kernel(chunks, steps, freq_count, load, tiles_hbm, x_ref, w_ref, t_hbm, *refs):
    outs, refs = refs[: len(chunks)], refs[len(chunks) :]
    if load:
        x_hbm, w_hbm, xbuf, wbuf = x_ref, w_ref, refs[0], refs[1]
        refs = refs[2:]
    else:
        xbuf, wbuf = x_ref, w_ref
    tiles, tbuf, table, spectra, tilesem, xsem, wsem, tsem = refs
    shots_here, blocks_here, block_len, tile_len = wbuf.shape
    me_shot, me_freq = lax.axis_index("shot"), lax.axis_index("freq")
    rows = t_hbm.shape[2]
    groups = [g for chunk in chunks for g in chunk]
    place, stride, start = {}, {}, 0
    for chunk in chunks:
        for j, g in enumerate(chunk):
            place[g], stride[g] = start + j * rows, len(chunk) * rows
        start += len(chunk) * freq_count * rows

    def x_copy(i):
        return pltpu.make_async_copy(x_hbm.at[i], xbuf.at[i], xsem.at[i])

    def w_copy(i):
        return pltpu.make_async_copy(w_hbm.at[i, pl.ds(me_freq * blocks_here, blocks_here)], wbuf.at[i], wsem.at[i])

    def t_copy(i):
        return pltpu.make_async_copy(t_hbm.at[:, jnp.bitwise_xor(me_freq, i)], tbuf.at[:, i], tsem.at[i])

    tile_copy = pltpu.make_async_copy(tiles_hbm, tiles, tilesem)
    tile_copy.start()
    for i in range(freq_count):
        t_copy(i).start()
    if load:
        x_copy(0).start()
        w_copy(0).start()
        for i in range(1, DEPTH):
            x_copy(i).start()
    for out in outs:
        out[...] = jnp.zeros_like(out)
    tile_copy.wait()
    for i in range(freq_count):
        t_copy(i).wait()
    for n in range(len(groups)):
        high, low = split(jnp.concatenate([tbuf[n, i] for i in range(freq_count)], axis=0))
        table[n] = jnp.concatenate([high, low], axis=0)

    def transform(i, n, part):
        high, low = split(part)
        wide = dot_nt(table[n], high)
        half = wide.shape[0] // 2
        result = wide[:half] + wide[half:] + dot_nt(table[n, :half], low)
        g = groups[n]
        for j in range(freq_count):
            start = place[g] + j * stride[g]
            spectra[i % 2, start : start + rows] = result[j * rows : (j + 1) * rows]

    def spread(i, b):
        if load and b == 0:
            w_copy(i).wait()
        s_high, s_low = split(spectra[i % 2, :, b * block_len : (b + 1) * block_len])
        w_high, w_low = split(wbuf[i, b])
        weights = jnp.concatenate(
            [
                jnp.concatenate([w_high, w_low], axis=1),
                jnp.concatenate([w_high, jnp.zeros_like(w_low)], axis=1),
            ],
            axis=0,
        )
        both = jnp.dot(jnp.concatenate([s_high, s_low], axis=1), weights, preferred_element_type=jnp.float32)
        value = both[:, :tile_len] + both[:, tile_len:]
        tile = tiles[i, me_freq * blocks_here + b]
        start = 0
        for out, orders in zip(outs, steps):
            for slot in slots_of(tile, me_shot, orders, freq_count):
                out[slot] += value[start : start + out.shape[1]]
                start += out.shape[1]

    for i in range(shots_here + 1):
        folded = ()
        if i < shots_here:
            if load:
                x_copy(i).wait()
                if i + DEPTH < shots_here:
                    x_copy(i + DEPTH).start()
                if i + 1 < shots_here:
                    w_copy(i + 1).start()
            folded = fold(xbuf[i], groups)
        for k in range(max(len(folded), blocks_here)):
            if k < len(folded):
                transform(i, k, folded[k])
            if i and k < blocks_here:
                spread(i - 1, k)


def bin_blocks(tile_ids, traces, interp_weights, chunks, steps, shot_count, freq_count, load, keep):
    shots_here, recs_here, time_len = traces.shape
    block_len, tile_len = interp_weights.shape[2:]
    blocks_here = recs_here // block_len
    groups = [g for chunk in chunks for g in chunk]
    tables = jnp.asarray(dft_tables(groups, freq_count, time_len))
    rows = freq_count * tables.shape[2]
    slot_count = shot_count * freq_count * TILES_DEV
    kept = [
        jax.ShapeDtypeStruct(traces.shape, jnp.float32),
        jax.ShapeDtypeStruct((shots_here, blocks_here, block_len, tile_len), jnp.float32),
    ]
    total = slot_count * len(GROUPS) * tables.shape[2] * tile_len * 4
    sums = pltpu.VMEM if total <= VMEM_SUMS else jax.ShapeDtypeStruct
    out_shape = [sums((slot_count, tables.shape[2] * len(chunk), tile_len), jnp.float32) for chunk in chunks]
    scratch = [
        pltpu.SMEM(tile_ids.shape, jnp.int32),
        pltpu.VMEM(tables.shape, jnp.float32),
        pltpu.VMEM((len(groups), 2 * rows, tables.shape[3]), jnp.bfloat16),
        pltpu.VMEM((2, len(groups) * rows, recs_here), jnp.float32),
        pltpu.SemaphoreType.DMA,
        pltpu.SemaphoreType.DMA((shots_here,)),
        pltpu.SemaphoreType.DMA((shots_here,)),
        pltpu.SemaphoreType.DMA((freq_count,)),
    ]
    if load and keep:
        out_shape += [pltpu.VMEM(k.shape, k.dtype) for k in kept]
    elif load:
        scratch = [pltpu.VMEM(k.shape, k.dtype) for k in kept] + scratch
    place = pltpu.HBM if load else pltpu.VMEM

    def body(*refs):
        bin_kernel(chunks, steps, freq_count, load, *refs)

    tile_ids = pltpu.with_memory_space_constraint(tile_ids, pltpu.HBM)
    traces = pltpu.with_memory_space_constraint(traces, place)
    interp_weights = pltpu.with_memory_space_constraint(interp_weights, place)
    tables = pltpu.with_memory_space_constraint(tables, pltpu.HBM)
    return pl.pallas_call(
        body,
        in_specs=[
            pl.BlockSpec(memory_space=pltpu.HBM),
            pl.BlockSpec(memory_space=place),
            pl.BlockSpec(memory_space=place),
            pl.BlockSpec(memory_space=pltpu.HBM),
        ],
        out_specs=[pl.BlockSpec(memory_space=pltpu.VMEM)] * len(out_shape),
        out_shape=out_shape,
        scratch_shapes=scratch,
        compiler_params=pltpu.CompilerParams(vmem_limit_bytes=VMEM_LIMIT),
        name="bin_blocks",
    )(tile_ids, traces, interp_weights, tables)


def shards(traces, interp_weights, tile_ids):
    shot_count = lax.axis_size("shot")
    freq_count = lax.axis_size("freq")
    tile_len = interp_weights.shape[3]
    steps = halvings(shot_count, freq_count)

    def halve(value, ways):
        pairs = []
        for shot in range(shot_count):
            for freq in range(freq_count):
                axis, bit = ways[shot & 1]
                to = (shot ^ (1 << bit), freq) if axis == "shot" else (shot, freq ^ (1 << bit))
                pairs.append((shot * freq_count + freq, to[0] * freq_count + to[1]))
        half = value.shape[0] // 2
        return value[:half] + lax.ppermute(value[half:], ("shot", "freq"), pairs)

    sums = [None] * len(CHUNKS)
    for n, call in enumerate(CALLS):
        chunks = tuple(CHUNKS[c] for c in call)
        made = bin_blocks(
            tile_ids,
            traces,
            interp_weights,
            chunks,
            [steps[c] for c in call],
            shot_count,
            freq_count,
            n == 0,
            n == 0 and len(CALLS) > 1,
        )
        for c, value in zip(call, made):
            sums[c] = value
        if len(made) > len(call):
            traces, interp_weights = made[len(call) :]
    parts = [None] * len(GROUPS)
    for chunk, orders, value in zip(CHUNKS, steps, sums):
        for ways in [(("shot", 0), ("shot", 0)), *zip(*orders)]:
            value = halve(value, ways)
        value = value.reshape(TILES_DEV, len(chunk), -1, tile_len)
        for j, g in enumerate(chunk):
            parts[g] = value[:, j]
    eighths = {}
    for g, residues in enumerate(GROUPS):
        if residues[0] % 2 == 0:
            part = parts[g].reshape(TILES_DEV, 2, -1, 2, tile_len)
            for j, residue in enumerate(residues):
                eighths[residue] = part[:, :, :, j]
        else:
            part = parts[g].reshape(TILES_DEV, 2, 2, -1, tile_len)
            for j, residue in enumerate(residues):
                eighths[residue] = part[:, j]
    return jnp.stack([eighths[r] for r in range(8)], axis=3).reshape(TILES_DEV, 2, -1, tile_len)


def solution(mesh):
    in_specs = (P("shot", "freq", None), P("shot", None, None, None), P("shot", None))
    out_specs = P("shot", None, "freq", None)
    return jax.shard_map(shards, mesh=mesh, in_specs=in_specs, out_specs=out_specs, check_vma=False)
```

```python
import math

import jax
import jax.numpy as jnp
import numpy as np
from jax import lax
from jax.experimental import pallas as pl
from jax.experimental.pallas import tpu as pltpu
from jax.sharding import PartitionSpec as P

NF = 384
TILES_DEV = 2
GROUPS = ((0, 4), (2, 6), (1, 7), (3, 5))
CHUNKS = ((0, 1), (2, 3))
ORDERS = (("axyb", "yaxb"), ("xayb", "yaxb"))
CALLS = ((0,), (1,))
DEPTH = 2
VMEM_SUMS = 16 << 20
VMEM_LIMIT = 24 << 20


def halvings(shot_count, freq_count):
    shot_bits = [("shot", bit) for bit in range(1, shot_count.bit_length() - 1)]
    freq_bits = [("freq", bit) for bit in range(freq_count.bit_length() - 1)]
    x, a = len(shot_bits) // 2, len(freq_bits) // 2
    steps = dict(x=shot_bits[:x], y=shot_bits[x:], a=freq_bits[:a], b=freq_bits[a:])
    return [[[step for name in order for step in steps[name]] for order in orders] for orders in ORDERS]


def dft_tables(groups, freq_count, time_len):
    freq_here = NF // freq_count
    scale = 1.0 / math.sqrt(time_len)
    tables = []
    for g in groups:
        residues = GROUPS[g]
        rows = []
        for owner in range(freq_count):
            if residues[0] % 2 == 0:
                freqs = owner * freq_here + np.arange(residues[0], freq_here, 4)
                angle = 2.0 * math.pi / time_len * (freqs[:, None] * np.arange(time_len // 4) % time_len)
                rows += [np.cos(angle), -np.sin(angle)]
            else:
                for residue in residues:
                    freqs = owner * freq_here + np.arange(residue, freq_here, 8)
                    angle = 2.0 * math.pi / time_len * (freqs[:, None] * np.arange(time_len // 8) % time_len)
                    cos, sin = np.cos(angle), np.sin(angle)
                    sign = 1.0 if residue in (1, 5) else -1.0
                    rows += [np.hstack([cos, -sign * sin]), np.hstack([-sin, -sign * cos])]
        tables.append((np.concatenate(rows) * scale).reshape(freq_count, -1, time_len // 4))
    return np.stack(tables).astype(np.float32)


def fold(x, groups):
    eighth = x.shape[1] // 8
    q0, q1, q2, q3 = (x[:, 2 * i * eighth : 2 * (i + 1) * eighth] for i in range(4))
    folded = {}
    if 0 in groups or 1 in groups:
        plus, cross = q0 + q2, q1 + q3
        folded[0], folded[1] = plus + cross, plus - cross
    if 2 in groups or 3 in groups:
        d02, d13 = q0 - q2, q1 - q3
        d0, d1, d2, d3 = d02[:, :eighth], d02[:, eighth:], d13[:, :eighth], d13[:, eighth:]
        root = math.sqrt(0.5)
        near, far = (d1 - d3) * root, (d1 + d3) * root
        folded[2] = jnp.concatenate([d0 + near, d2 + far], axis=1)
        folded[3] = jnp.concatenate([d0 - near, d2 - far], axis=1)
    return [folded[g] for g in groups]


def split(value):
    high = value.astype(jnp.bfloat16)
    return high, (value - high.astype(jnp.float32)).astype(jnp.bfloat16)


def dot_nt(a, b):
    return lax.dot_general(a, b, (((1,), (1,)), ((), ())), preferred_element_type=jnp.float32)


def slots_of(tile, me_shot, steps, freq_count):
    owner = tile // TILES_DEV
    apart = jnp.bitwise_xor(owner, me_shot)
    second = jnp.bitwise_and(owner, 1) == 1
    count = len(steps[0])
    base = jnp.bitwise_and(apart, 1) << count
    for axis, bit in steps[0]:
        if axis == "shot":
            flag = jnp.bitwise_and(jnp.right_shift(apart, bit), 1)
            places = [count - 1 - order.index((axis, bit)) for order in steps]
            base += jnp.where(second, flag << places[1], flag << places[0])
    slots = []
    for far in range(freq_count):
        places = [
            sum((far >> bit & 1) << (count - 1 - i) for i, (axis, bit) in enumerate(order) if axis == "freq")
            for order in steps
        ]
        slots.append((base + jnp.where(second, places[1], places[0])) * TILES_DEV + tile % TILES_DEV)
    return slots


def bin_kernel(chunks, steps, freq_count, load, tiles_hbm, x_ref, w_ref, t_ref, *refs):
    outs, refs = refs[: len(chunks)], refs[len(chunks) :]
    if load:
        x_hbm, w_hbm, xbuf, wbuf = x_ref, w_ref, refs[0], refs[1]
        refs = refs[2:]
    else:
        xbuf, wbuf = x_ref, w_ref
    tiles, tbuf, table, spectra, tilesem, xsem, wsem, tsem = refs
    shots_here, blocks_here, block_len, tile_len = wbuf.shape
    me_shot, me_freq = lax.axis_index("shot"), lax.axis_index("freq")
    rows = t_ref.shape[2]
    groups = [g for chunk in chunks for g in chunk]
    place, stride, start = {}, {}, 0
    for chunk in chunks:
        for j, g in enumerate(chunk):
            place[g], stride[g] = start + j * rows, len(chunk) * rows
        start += len(chunk) * freq_count * rows

    def x_copy(i):
        return pltpu.make_async_copy(x_hbm.at[i], xbuf.at[i], xsem.at[i])

    def w_copy(i):
        return pltpu.make_async_copy(w_hbm.at[i, pl.ds(me_freq * blocks_here, blocks_here)], wbuf.at[i], wsem.at[i])

    def t_copy(i):
        return pltpu.make_async_copy(t_ref.at[:, jnp.bitwise_xor(me_freq, i)], tbuf.at[:, i], tsem.at[i])

    def near_table(n, i):
        return tbuf[n, i] if load else t_ref[n, jnp.bitwise_xor(me_freq, i)]

    tile_copy = pltpu.make_async_copy(tiles_hbm, tiles, tilesem)
    tile_copy.start()
    if load:
        for i in range(freq_count):
            t_copy(i).start()
        x_copy(0).start()
        w_copy(0).start()
        for i in range(1, DEPTH):
            x_copy(i).start()
    for out in outs:
        out[...] = jnp.zeros_like(out)
    if load:
        for i in range(freq_count):
            t_copy(i).wait()
    for n in range(len(groups)):
        high, low = split(jnp.concatenate([near_table(n, i) for i in range(freq_count)], axis=0))
        table[n] = jnp.concatenate([high, low], axis=0)

    def transform(i, n, part):
        high, low = split(part)
        wide = dot_nt(table[n], high)
        half = wide.shape[0] // 2
        result = wide[:half] + wide[half:] + dot_nt(table[n, :half], low)
        g = groups[n]
        for j in range(freq_count):
            start = place[g] + j * stride[g]
            spectra[i % 2, start : start + rows] = result[j * rows : (j + 1) * rows]

    def spread(i, b):
        if load and b == 0:
            w_copy(i).wait()
        if i == 0 and b == 0:
            tile_copy.wait()
        s_high, s_low = split(spectra[i % 2, :, b * block_len : (b + 1) * block_len])
        w_high, w_low = split(wbuf[i, b])
        weights = jnp.concatenate(
            [
                jnp.concatenate([w_high, w_low], axis=1),
                jnp.concatenate([w_high, jnp.zeros_like(w_low)], axis=1),
            ],
            axis=0,
        )
        both = jnp.dot(jnp.concatenate([s_high, s_low], axis=1), weights, preferred_element_type=jnp.float32)
        value = both[:, :tile_len] + both[:, tile_len:]
        tile = tiles[i, me_freq * blocks_here + b]
        start = 0
        for out, orders in zip(outs, steps):
            for slot in slots_of(tile, me_shot, orders, freq_count):
                out[slot] += value[start : start + out.shape[1]]
                start += out.shape[1]

    for i in range(shots_here + 1):
        folded = ()
        if i < shots_here:
            if load:
                x_copy(i).wait()
                if i + DEPTH < shots_here:
                    x_copy(i + DEPTH).start()
                if i + 1 < shots_here:
                    w_copy(i + 1).start()
            folded = fold(xbuf[i], groups)
        for k in range(max(len(folded), blocks_here)):
            if k < len(folded):
                transform(i, k, folded[k])
            if i and k < blocks_here:
                spread(i - 1, k)


def bin_blocks(tile_ids, traces, interp_weights, chunks, steps, shot_count, freq_count, load, keep):
    shots_here, recs_here, time_len = traces.shape
    block_len, tile_len = interp_weights.shape[2:]
    blocks_here = recs_here // block_len
    groups = [g for chunk in chunks for g in chunk]
    tables = jnp.asarray(dft_tables(groups, freq_count, time_len))
    rows = freq_count * tables.shape[2]
    slot_count = shot_count * freq_count * TILES_DEV
    kept = [
        jax.ShapeDtypeStruct(traces.shape, jnp.float32),
        jax.ShapeDtypeStruct((shots_here, blocks_here, block_len, tile_len), jnp.float32),
    ]
    total = slot_count * len(GROUPS) * tables.shape[2] * tile_len * 4
    sums = pltpu.VMEM if total <= VMEM_SUMS else jax.ShapeDtypeStruct
    out_shape = [sums((slot_count, tables.shape[2] * len(chunk), tile_len), jnp.float32) for chunk in chunks]
    scratch = [
        pltpu.SMEM(tile_ids.shape, jnp.int32),
        pltpu.VMEM(tables.shape, jnp.float32),
        pltpu.VMEM((len(groups), 2 * rows, tables.shape[3]), jnp.bfloat16),
        pltpu.VMEM((2, len(groups) * rows, recs_here), jnp.float32),
        pltpu.SemaphoreType.DMA,
        pltpu.SemaphoreType.DMA((shots_here,)),
        pltpu.SemaphoreType.DMA((shots_here,)),
        pltpu.SemaphoreType.DMA((freq_count,)),
    ]
    if load and keep:
        out_shape += [pltpu.VMEM(k.shape, k.dtype) for k in kept]
    elif load:
        scratch = [pltpu.VMEM(k.shape, k.dtype) for k in kept] + scratch
    place = pltpu.HBM if load else pltpu.VMEM

    def body(*refs):
        bin_kernel(chunks, steps, freq_count, load, *refs)

    tile_ids = pltpu.with_memory_space_constraint(tile_ids, pltpu.HBM)
    traces = pltpu.with_memory_space_constraint(traces, place)
    interp_weights = pltpu.with_memory_space_constraint(interp_weights, place)
    tables = pltpu.with_memory_space_constraint(tables, place)
    return pl.pallas_call(
        body,
        in_specs=[
            pl.BlockSpec(memory_space=pltpu.HBM),
            pl.BlockSpec(memory_space=place),
            pl.BlockSpec(memory_space=place),
            pl.BlockSpec(memory_space=place),
        ],
        out_specs=[pl.BlockSpec(memory_space=pltpu.VMEM)] * len(out_shape),
        out_shape=out_shape,
        scratch_shapes=scratch,
        compiler_params=pltpu.CompilerParams(vmem_limit_bytes=VMEM_LIMIT),
        name="bin_blocks",
    )(tile_ids, traces, interp_weights, tables)


def assemble_kernel(*refs):
    out = refs[-1]
    freq_here = out.shape[2]
    for n, chunk in enumerate(CHUNKS):
        rows = refs[2 * n].shape[1] // len(chunk)
        for tile in range(TILES_DEV):
            value = refs[2 * n][tile] + refs[2 * n + 1][tile]
            for j, g in enumerate(chunk):
                stride = 4 if GROUPS[g][0] % 2 == 0 else 8
                residues = GROUPS[g][:1] if stride == 4 else GROUPS[g]
                size = freq_here // stride
                start = j * rows
                for residue in residues:
                    for part in range(2):
                        out[tile, part, pl.ds(residue, size, stride)] = value[start : start + size]
                        start += size


def assemble(last, freq_here, tile_len):
    last = [pltpu.with_memory_space_constraint(value, pltpu.VMEM) for value in last]
    return pl.pallas_call(
        assemble_kernel,
        in_specs=[pl.BlockSpec(memory_space=pltpu.VMEM)] * len(last),
        out_specs=pl.BlockSpec(memory_space=pltpu.VMEM),
        out_shape=jax.ShapeDtypeStruct((TILES_DEV, 2, freq_here, tile_len), jnp.float32),
        name="assemble",
    )(*last)


def shards(traces, interp_weights, tile_ids):
    shot_count = lax.axis_size("shot")
    freq_count = lax.axis_size("freq")
    tile_len = interp_weights.shape[3]
    steps = halvings(shot_count, freq_count)

    def halve(value, ways):
        pairs = []
        for shot in range(shot_count):
            for freq in range(freq_count):
                axis, bit = ways[shot & 1]
                to = (shot ^ (1 << bit), freq) if axis == "shot" else (shot, freq ^ (1 << bit))
                pairs.append((shot * freq_count + freq, to[0] * freq_count + to[1]))
        half = value.shape[0] // 2
        return value[:half], lax.ppermute(value[half:], ("shot", "freq"), pairs)

    sums = [None] * len(CHUNKS)
    for n, call in enumerate(CALLS):
        chunks = tuple(CHUNKS[c] for c in call)
        made = bin_blocks(
            tile_ids,
            traces,
            interp_weights,
            chunks,
            [steps[c] for c in call],
            shot_count,
            freq_count,
            n == 0,
            n == 0 and len(CALLS) > 1,
        )
        for c, value in zip(call, made):
            sums[c] = value
        if len(made) > len(call):
            traces, interp_weights = made[len(call) :]
    last = []
    for orders, value in zip(steps, sums):
        for ways in [(("shot", 0), ("shot", 0)), *zip(*orders)]:
            kept, got = halve(value, ways)
            value = kept + got
        last += [kept, got]
    return assemble(last, NF // freq_count, tile_len)


def solution(mesh):
    in_specs = (P("shot", "freq", None), P("shot", None, None, None), P("shot", None))
    out_specs = P("shot", None, "freq", None)
    return jax.shard_map(shards, mesh=mesh, in_specs=in_specs, out_specs=out_specs, check_vma=False)
```

```python
import math

import jax
import jax.numpy as jnp
import numpy as np
from jax import lax
from jax.experimental import pallas as pl
from jax.experimental.pallas import tpu as pltpu
from jax.sharding import PartitionSpec as P

NF = 384
TILES_DEV = 2
GROUPS = ((0, 4), (2, 6), (1, 7), (3, 5))
CHUNKS = ((0, 1), (2, 3))
ORDERS = (("axyb", "yabx"), ("xayb", "yxab"))
CALLS = ((0,), (1,))
DEPTH = 2
VMEM_SUMS = 16 << 20
VMEM_LIMIT = 24 << 20


def halvings(shot_count, freq_count):
    shot_bits = [("shot", bit) for bit in range(1, shot_count.bit_length() - 1)]
    freq_bits = [("freq", bit) for bit in range(freq_count.bit_length() - 1)]
    x, a = len(shot_bits) // 2, len(freq_bits) // 2
    steps = dict(x=shot_bits[:x], y=shot_bits[x:], a=freq_bits[:a], b=freq_bits[a:])
    return [[[step for name in order for step in steps[name]] for order in orders] for orders in ORDERS]


def dft_tables(groups, freq_count, time_len):
    freq_here = NF // freq_count
    scale = 1.0 / math.sqrt(time_len)
    tables = []
    for g in groups:
        residues = GROUPS[g]
        rows = []
        for owner in range(freq_count):
            if residues[0] % 2 == 0:
                freqs = owner * freq_here + np.arange(residues[0], freq_here, 4)
                angle = 2.0 * math.pi / time_len * (freqs[:, None] * np.arange(time_len // 4) % time_len)
                rows += [np.cos(angle), -np.sin(angle)]
            else:
                for residue in residues:
                    freqs = owner * freq_here + np.arange(residue, freq_here, 8)
                    angle = 2.0 * math.pi / time_len * (freqs[:, None] * np.arange(time_len // 8) % time_len)
                    cos, sin = np.cos(angle), np.sin(angle)
                    sign = 1.0 if residue in (1, 5) else -1.0
                    rows += [np.hstack([cos, -sign * sin]), np.hstack([-sin, -sign * cos])]
        tables.append((np.concatenate(rows) * scale).reshape(freq_count, -1, time_len // 4))
    return np.stack(tables).astype(np.float32)


def fold(x, groups):
    eighth = x.shape[1] // 8
    q0, q1, q2, q3 = (x[:, 2 * i * eighth : 2 * (i + 1) * eighth] for i in range(4))
    folded = {}
    if 0 in groups or 1 in groups:
        plus, cross = q0 + q2, q1 + q3
        folded[0], folded[1] = plus + cross, plus - cross
    if 2 in groups or 3 in groups:
        d02, d13 = q0 - q2, q1 - q3
        d0, d1, d2, d3 = d02[:, :eighth], d02[:, eighth:], d13[:, :eighth], d13[:, eighth:]
        root = math.sqrt(0.5)
        near, far = (d1 - d3) * root, (d1 + d3) * root
        folded[2] = jnp.concatenate([d0 + near, d2 + far], axis=1)
        folded[3] = jnp.concatenate([d0 - near, d2 - far], axis=1)
    return [folded[g] for g in groups]


def split(value):
    high = value.astype(jnp.bfloat16)
    return high, (value - high.astype(jnp.float32)).astype(jnp.bfloat16)


def dot_nt(a, b):
    return lax.dot_general(a, b, (((1,), (1,)), ((), ())), preferred_element_type=jnp.float32)


def slots_of(tile, me_shot, steps, freq_count):
    owner = tile // TILES_DEV
    apart = jnp.bitwise_xor(owner, me_shot)
    second = jnp.bitwise_and(owner, 1) == 1
    count = len(steps[0])
    base = jnp.bitwise_and(apart, 1) << count
    for axis, bit in steps[0]:
        if axis == "shot":
            flag = jnp.bitwise_and(jnp.right_shift(apart, bit), 1)
            places = [count - 1 - order.index((axis, bit)) for order in steps]
            base += jnp.where(second, flag << places[1], flag << places[0])
    slots = []
    for far in range(freq_count):
        places = [
            sum((far >> bit & 1) << (count - 1 - i) for i, (axis, bit) in enumerate(order) if axis == "freq")
            for order in steps
        ]
        slots.append((base + jnp.where(second, places[1], places[0])) * TILES_DEV + tile % TILES_DEV)
    return slots


def bin_kernel(chunks, steps, freq_count, load, tiles_hbm, x_ref, w_ref, t_ref, *refs):
    outs, refs = refs[: len(chunks)], refs[len(chunks) :]
    if load:
        x_hbm, w_hbm, xbuf, wbuf = x_ref, w_ref, refs[0], refs[1]
        refs = refs[2:]
    else:
        xbuf, wbuf = x_ref, w_ref
    tiles, tbuf, table, spectra, tilesem, xsem, wsem, tsem = refs
    shots_here, blocks_here, block_len, tile_len = wbuf.shape
    me_shot, me_freq = lax.axis_index("shot"), lax.axis_index("freq")
    rows = t_ref.shape[2]
    groups = [g for chunk in chunks for g in chunk]
    place, stride, start = {}, {}, 0
    for chunk in chunks:
        for j, g in enumerate(chunk):
            place[g], stride[g] = start + j * rows, len(chunk) * rows
        start += len(chunk) * freq_count * rows

    def x_copy(i):
        return pltpu.make_async_copy(x_hbm.at[i], xbuf.at[i], xsem.at[i])

    def w_copy(i):
        return pltpu.make_async_copy(w_hbm.at[i, pl.ds(me_freq * blocks_here, blocks_here)], wbuf.at[i], wsem.at[i])

    def t_copy(i):
        return pltpu.make_async_copy(t_ref.at[:, jnp.bitwise_xor(me_freq, i)], tbuf.at[:, i], tsem.at[i])

    def near_table(n, i):
        return tbuf[n, i] if load else t_ref[n, jnp.bitwise_xor(me_freq, i)]

    tile_copy = pltpu.make_async_copy(tiles_hbm, tiles, tilesem)
    tile_copy.start()
    if load:
        for i in range(freq_count):
            t_copy(i).start()
        x_copy(0).start()
        w_copy(0).start()
        for i in range(1, DEPTH):
            x_copy(i).start()
    for out in outs:
        out[...] = jnp.zeros_like(out)
    if load:
        for i in range(freq_count):
            t_copy(i).wait()
    for n in range(len(groups)):
        high, low = split(jnp.concatenate([near_table(n, i) for i in range(freq_count)], axis=0))
        table[n] = jnp.concatenate([high, low], axis=0)

    def transform(i, n, part):
        high, low = split(part)
        wide = dot_nt(table[n], high)
        half = wide.shape[0] // 2
        result = wide[:half] + wide[half:] + dot_nt(table[n, :half], low)
        g = groups[n]
        for j in range(freq_count):
            start = place[g] + j * stride[g]
            spectra[i % 2, start : start + rows] = result[j * rows : (j + 1) * rows]

    def spread(i, b):
        if load and b == 0:
            w_copy(i).wait()
        if i == 0 and b == 0:
            tile_copy.wait()
        s_high, s_low = split(spectra[i % 2, :, b * block_len : (b + 1) * block_len])
        w_high, w_low = split(wbuf[i, b])
        weights = jnp.concatenate(
            [
                jnp.concatenate([w_high, w_low], axis=1),
                jnp.concatenate([w_high, jnp.zeros_like(w_low)], axis=1),
            ],
            axis=0,
        )
        both = jnp.dot(jnp.concatenate([s_high, s_low], axis=1), weights, preferred_element_type=jnp.float32)
        value = both[:, :tile_len] + both[:, tile_len:]
        tile = tiles[i, me_freq * blocks_here + b]
        start = 0
        for out, orders in zip(outs, steps):
            for slot in slots_of(tile, me_shot, orders, freq_count):
                out[slot] += value[start : start + out.shape[1]]
                start += out.shape[1]

    for i in range(shots_here + 1):
        folded = ()
        if i < shots_here:
            if load:
                x_copy(i).wait()
                if i + DEPTH < shots_here:
                    x_copy(i + DEPTH).start()
                if i + 1 < shots_here:
                    w_copy(i + 1).start()
            folded = fold(xbuf[i], groups)
        for k in range(max(len(folded), blocks_here)):
            if k < len(folded):
                transform(i, k, folded[k])
            if i and k < blocks_here:
                spread(i - 1, k)


def bin_blocks(tile_ids, traces, interp_weights, chunks, steps, shot_count, freq_count, load, keep):
    shots_here, recs_here, time_len = traces.shape
    block_len, tile_len = interp_weights.shape[2:]
    blocks_here = recs_here // block_len
    groups = [g for chunk in chunks for g in chunk]
    tables = jnp.asarray(dft_tables(groups, freq_count, time_len))
    rows = freq_count * tables.shape[2]
    slot_count = shot_count * freq_count * TILES_DEV
    kept = [
        jax.ShapeDtypeStruct(traces.shape, jnp.float32),
        jax.ShapeDtypeStruct((shots_here, blocks_here, block_len, tile_len), jnp.float32),
    ]
    total = slot_count * len(GROUPS) * tables.shape[2] * tile_len * 4
    sums = pltpu.VMEM if total <= VMEM_SUMS else jax.ShapeDtypeStruct
    out_shape = [sums((slot_count, tables.shape[2] * len(chunk), tile_len), jnp.float32) for chunk in chunks]
    scratch = [
        pltpu.SMEM(tile_ids.shape, jnp.int32),
        pltpu.VMEM(tables.shape, jnp.float32),
        pltpu.VMEM((len(groups), 2 * rows, tables.shape[3]), jnp.bfloat16),
        pltpu.VMEM((2, len(groups) * rows, recs_here), jnp.float32),
        pltpu.SemaphoreType.DMA,
        pltpu.SemaphoreType.DMA((shots_here,)),
        pltpu.SemaphoreType.DMA((shots_here,)),
        pltpu.SemaphoreType.DMA((freq_count,)),
    ]
    if load and keep:
        out_shape += [pltpu.VMEM(k.shape, k.dtype) for k in kept]
    elif load:
        scratch = [pltpu.VMEM(k.shape, k.dtype) for k in kept] + scratch
    place = pltpu.HBM if load else pltpu.VMEM

    def body(*refs):
        bin_kernel(chunks, steps, freq_count, load, *refs)

    tile_ids = pltpu.with_memory_space_constraint(tile_ids, pltpu.HBM)
    traces = pltpu.with_memory_space_constraint(traces, place)
    interp_weights = pltpu.with_memory_space_constraint(interp_weights, place)
    tables = pltpu.with_memory_space_constraint(tables, place)
    return pl.pallas_call(
        body,
        in_specs=[
            pl.BlockSpec(memory_space=pltpu.HBM),
            pl.BlockSpec(memory_space=place),
            pl.BlockSpec(memory_space=place),
            pl.BlockSpec(memory_space=place),
        ],
        out_specs=[pl.BlockSpec(memory_space=pltpu.VMEM)] * len(out_shape),
        out_shape=out_shape,
        scratch_shapes=scratch,
        compiler_params=pltpu.CompilerParams(vmem_limit_bytes=VMEM_LIMIT),
        name="bin_blocks",
    )(tile_ids, traces, interp_weights, tables)


def assemble_kernel(*refs):
    out = refs[-1]
    freq_here = out.shape[2]
    for n, chunk in enumerate(CHUNKS):
        rows = refs[2 * n].shape[1] // len(chunk)
        for tile in range(TILES_DEV):
            value = refs[2 * n][tile] + refs[2 * n + 1][tile]
            for j, g in enumerate(chunk):
                stride = 4 if GROUPS[g][0] % 2 == 0 else 8
                residues = GROUPS[g][:1] if stride == 4 else GROUPS[g]
                size = freq_here // stride
                start = j * rows
                for residue in residues:
                    for part in range(2):
                        out[tile, part, pl.ds(residue, size, stride)] = value[start : start + size]
                        start += size


def assemble(last, freq_here, tile_len):
    last = [pltpu.with_memory_space_constraint(value, pltpu.VMEM) for value in last]
    return pl.pallas_call(
        assemble_kernel,
        in_specs=[pl.BlockSpec(memory_space=pltpu.VMEM)] * len(last),
        out_specs=pl.BlockSpec(memory_space=pltpu.VMEM),
        out_shape=jax.ShapeDtypeStruct((TILES_DEV, 2, freq_here, tile_len), jnp.float32),
        name="assemble",
    )(*last)


def shards(traces, interp_weights, tile_ids):
    shot_count = lax.axis_size("shot")
    freq_count = lax.axis_size("freq")
    tile_len = interp_weights.shape[3]
    steps = halvings(shot_count, freq_count)

    def halve(value, ways):
        pairs = []
        for shot in range(shot_count):
            for freq in range(freq_count):
                axis, bit = ways[shot & 1]
                to = (shot ^ (1 << bit), freq) if axis == "shot" else (shot, freq ^ (1 << bit))
                pairs.append((shot * freq_count + freq, to[0] * freq_count + to[1]))
        half = value.shape[0] // 2
        return value[:half], lax.ppermute(value[half:], ("shot", "freq"), pairs)

    sums = [None] * len(CHUNKS)
    for n, call in enumerate(CALLS):
        chunks = tuple(CHUNKS[c] for c in call)
        made = bin_blocks(
            tile_ids,
            traces,
            interp_weights,
            chunks,
            [steps[c] for c in call],
            shot_count,
            freq_count,
            n == 0,
            n == 0 and len(CALLS) > 1,
        )
        for c, value in zip(call, made):
            sums[c] = value
        if len(made) > len(call):
            traces, interp_weights = made[len(call) :]
    last = []
    for orders, value in zip(steps, sums):
        for ways in [(("shot", 0), ("shot", 0)), *zip(*orders)]:
            kept, got = halve(value, ways)
            value = kept + got
        last += [kept, got]
    return assemble(last, NF // freq_count, tile_len)


def solution(mesh):
    in_specs = (P("shot", "freq", None), P("shot", None, None, None), P("shot", None))
    out_specs = P("shot", None, "freq", None)
    return jax.shard_map(shards, mesh=mesh, in_specs=in_specs, out_specs=out_specs, check_vma=False)
```

```python
import math

import jax
import jax.numpy as jnp
import numpy as np
from jax import lax
from jax.experimental import pallas as pl
from jax.experimental.pallas import tpu as pltpu
from jax.sharding import PartitionSpec as P

NF = 384
TILES_DEV = 2
GROUPS = ((0, 4), (2, 6), (1, 7), (3, 5))
CHUNKS = ((0, 1), (2, 3))
ORDERS = (("axyb", "yabx"), ("xayb", "yxab"))
CALLS = ((0,), (1,))
DEPTH = 2
VMEM_SUMS = 16 << 20
VMEM_LIMIT = 24 << 20


def halvings(shot_count, freq_count):
    shot_bits = [("shot", bit) for bit in range(1, shot_count.bit_length() - 1)]
    freq_bits = [("freq", bit) for bit in range(freq_count.bit_length() - 1)]
    x, a = len(shot_bits) // 2, len(freq_bits) // 2
    steps = dict(x=shot_bits[:x], y=shot_bits[x:], a=freq_bits[:a], b=freq_bits[a:])
    return [[[step for name in order for step in steps[name]] for order in orders] for orders in ORDERS]


def dft_tables(groups, freq_count, time_len):
    freq_here = NF // freq_count
    scale = 1.0 / math.sqrt(time_len)
    tables = []
    for g in groups:
        residues = GROUPS[g]
        rows = []
        for owner in range(freq_count):
            if residues[0] % 2 == 0:
                freqs = owner * freq_here + np.arange(residues[0], freq_here, 4)
                angle = 2.0 * math.pi / time_len * (freqs[:, None] * np.arange(time_len // 4) % time_len)
                rows += [np.cos(angle), -np.sin(angle)]
            else:
                for residue in residues:
                    freqs = owner * freq_here + np.arange(residue, freq_here, 8)
                    angle = 2.0 * math.pi / time_len * (freqs[:, None] * np.arange(time_len // 8) % time_len)
                    cos, sin = np.cos(angle), np.sin(angle)
                    sign = 1.0 if residue in (1, 5) else -1.0
                    rows += [np.hstack([cos, -sign * sin]), np.hstack([-sin, -sign * cos])]
        tables.append((np.concatenate(rows) * scale).reshape(freq_count, -1, time_len // 4))
    return np.stack(tables).astype(np.float32)


def fold(x, groups):
    eighth = x.shape[1] // 8
    q0, q1, q2, q3 = (x[:, 2 * i * eighth : 2 * (i + 1) * eighth] for i in range(4))
    folded = {}
    if 0 in groups or 1 in groups:
        plus, cross = q0 + q2, q1 + q3
        folded[0], folded[1] = plus + cross, plus - cross
    if 2 in groups or 3 in groups:
        d02, d13 = q0 - q2, q1 - q3
        d0, d1, d2, d3 = d02[:, :eighth], d02[:, eighth:], d13[:, :eighth], d13[:, eighth:]
        root = math.sqrt(0.5)
        near, far = (d1 - d3) * root, (d1 + d3) * root
        folded[2] = jnp.concatenate([d0 + near, d2 + far], axis=1)
        folded[3] = jnp.concatenate([d0 - near, d2 - far], axis=1)
    return [folded[g] for g in groups]


def split(value):
    high = value.astype(jnp.bfloat16)
    return high, (value - high.astype(jnp.float32)).astype(jnp.bfloat16)


def dot_nt(a, b):
    return lax.dot_general(a, b, (((1,), (1,)), ((), ())), preferred_element_type=jnp.float32)


def slots_of(tile, me_shot, steps, freq_count):
    owner = tile // TILES_DEV
    apart = jnp.bitwise_xor(owner, me_shot)
    second = jnp.bitwise_and(owner, 1) == 1
    count = len(steps[0])
    base = jnp.bitwise_and(apart, 1) << count
    for axis, bit in steps[0]:
        if axis == "shot":
            flag = jnp.bitwise_and(jnp.right_shift(apart, bit), 1)
            places = [count - 1 - order.index((axis, bit)) for order in steps]
            base += jnp.where(second, flag << places[1], flag << places[0])
    slots = []
    for far in range(freq_count):
        places = [
            sum((far >> bit & 1) << (count - 1 - i) for i, (axis, bit) in enumerate(order) if axis == "freq")
            for order in steps
        ]
        slots.append((base + jnp.where(second, places[1], places[0])) * TILES_DEV + tile % TILES_DEV)
    return slots


def bin_kernel(chunks, steps, freq_count, load, tiles_hbm, x_ref, w_ref, t_ref, *refs):
    if load:
        next_hbm, refs = refs[0], refs[1:]
    outs, refs = refs[: len(chunks)], refs[len(chunks) :]
    if load:
        x_hbm, w_hbm, xbuf, wbuf, nextbuf = x_ref, w_ref, *refs[:3]
        refs = refs[3:]
    else:
        xbuf, wbuf = x_ref, w_ref
    tiles, tbuf, table, spectra, tilesem, xsem, wsem, tsem, nextsem = refs
    shots_here, blocks_here, block_len, tile_len = wbuf.shape
    me_shot, me_freq = lax.axis_index("shot"), lax.axis_index("freq")
    rows = t_ref.shape[2]
    groups = [g for chunk in chunks for g in chunk]
    place, stride, start = {}, {}, 0
    for chunk in chunks:
        for j, g in enumerate(chunk):
            place[g], stride[g] = start + j * rows, len(chunk) * rows
        start += len(chunk) * freq_count * rows

    def x_copy(i):
        return pltpu.make_async_copy(x_hbm.at[i], xbuf.at[i], xsem.at[i])

    def w_copy(i):
        return pltpu.make_async_copy(w_hbm.at[i, pl.ds(me_freq * blocks_here, blocks_here)], wbuf.at[i], wsem.at[i])

    def t_copy(i):
        return pltpu.make_async_copy(t_ref.at[:, jnp.bitwise_xor(me_freq, i)], tbuf.at[:, i], tsem.at[i])

    def near_table(n, i):
        return tbuf[n, i] if load else t_ref[n, jnp.bitwise_xor(me_freq, i)]

    tile_copy = pltpu.make_async_copy(tiles_hbm, tiles, tilesem)
    tile_copy.start()
    if load:
        for i in range(freq_count):
            t_copy(i).start()
        x_copy(0).start()
        w_copy(0).start()
        for i in range(1, DEPTH):
            x_copy(i).start()
    for out in outs:
        out[...] = jnp.zeros_like(out)
    if load:
        for i in range(freq_count):
            t_copy(i).wait()
    for n in range(len(groups)):
        high, low = split(jnp.concatenate([near_table(n, i) for i in range(freq_count)], axis=0))
        table[n] = jnp.concatenate([high, low], axis=0)

    def transform(i, n, part):
        high, low = split(part)
        wide = dot_nt(table[n], high)
        half = wide.shape[0] // 2
        result = wide[:half] + wide[half:] + dot_nt(table[n, :half], low)
        g = groups[n]
        for j in range(freq_count):
            start = place[g] + j * stride[g]
            spectra[i % 2, start : start + rows] = result[j * rows : (j + 1) * rows]

    def spread(i, b):
        if load and b == 0:
            w_copy(i).wait()
        if i == 0 and b == 0:
            tile_copy.wait()
        s_high, s_low = split(spectra[i % 2, :, b * block_len : (b + 1) * block_len])
        w_high, w_low = split(wbuf[i, b])
        weights = jnp.concatenate(
            [
                jnp.concatenate([w_high, w_low], axis=1),
                jnp.concatenate([w_high, jnp.zeros_like(w_low)], axis=1),
            ],
            axis=0,
        )
        both = jnp.dot(jnp.concatenate([s_high, s_low], axis=1), weights, preferred_element_type=jnp.float32)
        value = both[:, :tile_len] + both[:, tile_len:]
        tile = tiles[i, me_freq * blocks_here + b]
        start = 0
        for out, orders in zip(outs, steps):
            for slot in slots_of(tile, me_shot, orders, freq_count):
                out[slot] += value[start : start + out.shape[1]]
                start += out.shape[1]

    for i in range(shots_here + 1):
        folded = ()
        if i < shots_here:
            if load:
                x_copy(i).wait()
                if i + DEPTH < shots_here:
                    x_copy(i + DEPTH).start()
                if i == shots_here - 1:
                    next_copy = pltpu.make_async_copy(next_hbm, nextbuf, nextsem)
                    next_copy.start()
                if i + 1 < shots_here:
                    w_copy(i + 1).start()
            folded = fold(xbuf[i], groups)
        for k in range(max(len(folded), blocks_here)):
            if k < len(folded):
                transform(i, k, folded[k])
            if i and k < blocks_here:
                spread(i - 1, k)
    if load:
        next_copy.wait()


def bin_blocks(tile_ids, traces, interp_weights, tables, chunks, steps, shot_count, freq_count, following):
    load = following is not None
    shots_here, recs_here, time_len = traces.shape
    block_len, tile_len = interp_weights.shape[2:]
    blocks_here = recs_here // block_len
    groups = [g for chunk in chunks for g in chunk]
    rows = freq_count * tables.shape[2]
    slot_count = shot_count * freq_count * TILES_DEV
    kept = [
        jax.ShapeDtypeStruct(traces.shape, jnp.float32),
        jax.ShapeDtypeStruct((shots_here, blocks_here, block_len, tile_len), jnp.float32),
    ]
    total = slot_count * len(GROUPS) * tables.shape[2] * tile_len * 4
    sums = pltpu.VMEM if total <= VMEM_SUMS else jax.ShapeDtypeStruct
    out_shape = [sums((slot_count, tables.shape[2] * len(chunk), tile_len), jnp.float32) for chunk in chunks]
    scratch = [
        pltpu.SMEM(tile_ids.shape, jnp.int32),
        pltpu.VMEM(tables.shape, jnp.float32),
        pltpu.VMEM((len(groups), 2 * rows, tables.shape[3]), jnp.bfloat16),
        pltpu.VMEM((2, len(groups) * rows, recs_here), jnp.float32),
        pltpu.SemaphoreType.DMA,
        pltpu.SemaphoreType.DMA((shots_here,)),
        pltpu.SemaphoreType.DMA((shots_here,)),
        pltpu.SemaphoreType.DMA((freq_count,)),
        pltpu.SemaphoreType.DMA,
    ]
    if load:
        out_shape += [pltpu.VMEM(k.shape, k.dtype) for k in [*kept, following]]
    place = pltpu.HBM if load else pltpu.VMEM

    def body(*refs):
        bin_kernel(chunks, steps, freq_count, load, *refs)

    tile_ids = pltpu.with_memory_space_constraint(tile_ids, pltpu.HBM)
    traces = pltpu.with_memory_space_constraint(traces, place)
    interp_weights = pltpu.with_memory_space_constraint(interp_weights, place)
    tables = pltpu.with_memory_space_constraint(tables, place)
    more = [pltpu.with_memory_space_constraint(following, pltpu.HBM)] if load else []
    return pl.pallas_call(
        body,
        in_specs=[
            pl.BlockSpec(memory_space=pltpu.HBM),
            pl.BlockSpec(memory_space=place),
            pl.BlockSpec(memory_space=place),
            pl.BlockSpec(memory_space=place),
        ]
        + [pl.BlockSpec(memory_space=pltpu.HBM)] * load,
        out_specs=[pl.BlockSpec(memory_space=pltpu.VMEM)] * len(out_shape),
        out_shape=out_shape,
        scratch_shapes=scratch,
        compiler_params=pltpu.CompilerParams(vmem_limit_bytes=VMEM_LIMIT),
        name="bin_blocks",
    )(tile_ids, traces, interp_weights, tables, *more)


def assemble_kernel(*refs):
    out = refs[-1]
    freq_here = out.shape[2]
    for n, chunk in enumerate(CHUNKS):
        rows = refs[2 * n].shape[1] // len(chunk)
        for tile in range(TILES_DEV):
            value = refs[2 * n][tile] + refs[2 * n + 1][tile]
            for j, g in enumerate(chunk):
                stride = 4 if GROUPS[g][0] % 2 == 0 else 8
                residues = GROUPS[g][:1] if stride == 4 else GROUPS[g]
                size = freq_here // stride
                start = j * rows
                for residue in residues:
                    for part in range(2):
                        out[tile, part, pl.ds(residue, size, stride)] = value[start : start + size]
                        start += size


def assemble(last, freq_here, tile_len):
    last = [pltpu.with_memory_space_constraint(value, pltpu.VMEM) for value in last]
    return pl.pallas_call(
        assemble_kernel,
        in_specs=[pl.BlockSpec(memory_space=pltpu.VMEM)] * len(last),
        out_specs=pl.BlockSpec(memory_space=pltpu.VMEM),
        out_shape=jax.ShapeDtypeStruct((TILES_DEV, 2, freq_here, tile_len), jnp.float32),
        name="assemble",
    )(*last)


def shards(traces, interp_weights, tile_ids):
    shot_count = lax.axis_size("shot")
    freq_count = lax.axis_size("freq")
    tile_len = interp_weights.shape[3]
    steps = halvings(shot_count, freq_count)

    def halve(value, ways):
        pairs = []
        for shot in range(shot_count):
            for freq in range(freq_count):
                axis, bit = ways[shot & 1]
                to = (shot ^ (1 << bit), freq) if axis == "shot" else (shot, freq ^ (1 << bit))
                pairs.append((shot * freq_count + freq, to[0] * freq_count + to[1]))
        half = value.shape[0] // 2
        return value[:half], lax.ppermute(value[half:], ("shot", "freq"), pairs)

    sums = [None] * len(CHUNKS)
    first, following = (
        jnp.asarray(dft_tables([g for c in call for g in CHUNKS[c]], freq_count, traces.shape[2])) for call in CALLS
    )
    for n, call in enumerate(CALLS):
        chunks = tuple(CHUNKS[c] for c in call)
        made = bin_blocks(
            tile_ids,
            traces,
            interp_weights,
            following if n else first,
            chunks,
            [steps[c] for c in call],
            shot_count,
            freq_count,
            None if n else following,
        )
        for c, value in zip(call, made):
            sums[c] = value
        if len(made) > len(call):
            traces, interp_weights, following = made[len(call) :]
    last = []
    for orders, value in zip(steps, sums):
        for ways in [(("shot", 0), ("shot", 0)), *zip(*orders)]:
            kept, got = halve(value, ways)
            value = kept + got
        last += [kept, got]
    return assemble(last, NF // freq_count, tile_len)


def solution(mesh):
    in_specs = (P("shot", "freq", None), P("shot", None, None, None), P("shot", None))
    out_specs = P("shot", None, "freq", None)
    return jax.shard_map(shards, mesh=mesh, in_specs=in_specs, out_specs=out_specs, check_vma=False)
```

```python
import math

import jax
import jax.numpy as jnp
import numpy as np
from jax import lax
from jax.experimental import pallas as pl
from jax.experimental.pallas import tpu as pltpu
from jax.sharding import PartitionSpec as P

NF = 384
TILES_DEV = 2
GROUPS = ((0, 4), (2, 6), (1, 7), (3, 5))
CHUNKS = ((0, 1), (2, 3))
ORDERS = (("axyb", "yabx"), ("xayb", "yxab"))
CALLS = ((0,), (1,))
DEPTH = 2
VMEM_SUMS = 16 << 20
VMEM_LIMIT = 24 << 20


def halvings(shot_count, freq_count):
    shot_bits = [("shot", bit) for bit in range(1, shot_count.bit_length() - 1)]
    freq_bits = [("freq", bit) for bit in range(freq_count.bit_length() - 1)]
    x, a = len(shot_bits) // 2, len(freq_bits) // 2
    steps = dict(x=shot_bits[:x], y=shot_bits[x:], a=freq_bits[:a], b=freq_bits[a:])
    return [[[step for name in order for step in steps[name]] for order in orders] for orders in ORDERS]


def dft_tables(groups, freq_count, time_len):
    freq_here = NF // freq_count
    scale = 1.0 / math.sqrt(time_len)
    tables = []
    for g in groups:
        residues = GROUPS[g]
        rows = []
        for owner in range(freq_count):
            if residues[0] % 2 == 0:
                freqs = owner * freq_here + np.arange(residues[0], freq_here, 4)
                angle = 2.0 * math.pi / time_len * (freqs[:, None] * np.arange(time_len // 4) % time_len)
                rows += [np.cos(angle), -np.sin(angle)]
            else:
                for residue in residues:
                    freqs = owner * freq_here + np.arange(residue, freq_here, 8)
                    angle = 2.0 * math.pi / time_len * (freqs[:, None] * np.arange(time_len // 8) % time_len)
                    cos, sin = np.cos(angle), np.sin(angle)
                    sign = 1.0 if residue in (1, 5) else -1.0
                    rows += [np.hstack([cos, -sign * sin]), np.hstack([-sin, -sign * cos])]
        tables.append((np.concatenate(rows) * scale).reshape(freq_count, -1, time_len // 4))
    return np.stack(tables).astype(np.float32)


def fold(x, groups):
    eighth = x.shape[1] // 8
    q0, q1, q2, q3 = (x[:, 2 * i * eighth : 2 * (i + 1) * eighth] for i in range(4))
    folded = {}
    if 0 in groups or 1 in groups:
        plus, cross = q0 + q2, q1 + q3
        folded[0], folded[1] = plus + cross, plus - cross
    if 2 in groups or 3 in groups:
        d02, d13 = q0 - q2, q1 - q3
        d0, d1, d2, d3 = d02[:, :eighth], d02[:, eighth:], d13[:, :eighth], d13[:, eighth:]
        root = math.sqrt(0.5)
        near, far = (d1 - d3) * root, (d1 + d3) * root
        folded[2] = jnp.concatenate([d0 + near, d2 + far], axis=1)
        folded[3] = jnp.concatenate([d0 - near, d2 - far], axis=1)
    return [folded[g] for g in groups]


def split(value):
    high = value.astype(jnp.bfloat16)
    return high, (value - high.astype(jnp.float32)).astype(jnp.bfloat16)


def dot_nt(a, b):
    return lax.dot_general(a, b, (((1,), (1,)), ((), ())), preferred_element_type=jnp.float32)


def slots_of(tile, me_shot, steps, freq_count):
    owner = tile // TILES_DEV
    apart = jnp.bitwise_xor(owner, me_shot)
    second = jnp.bitwise_and(owner, 1) == 1
    count = len(steps[0])
    base = jnp.bitwise_and(apart, 1) << count
    for axis, bit in steps[0]:
        if axis == "shot":
            flag = jnp.bitwise_and(jnp.right_shift(apart, bit), 1)
            places = [count - 1 - order.index((axis, bit)) for order in steps]
            base += jnp.where(second, flag << places[1], flag << places[0])
    slots = []
    for far in range(freq_count):
        places = [
            sum((far >> bit & 1) << (count - 1 - i) for i, (axis, bit) in enumerate(order) if axis == "freq")
            for order in steps
        ]
        slots.append((base + jnp.where(second, places[1], places[0])) * TILES_DEV + tile % TILES_DEV)
    return slots


def bin_kernel(chunks, steps, freq_count, load, tiles_hbm, x_ref, w_ref, t_ref, *refs):
    if load:
        next_hbm, refs = refs[0], refs[1:]
    outs, refs = refs[: len(chunks)], refs[len(chunks) :]
    if load:
        x_hbm, w_hbm, xbuf, wbuf, nextbuf = x_ref, w_ref, *refs[:3]
        refs = refs[3:]
    else:
        xbuf, wbuf = x_ref, w_ref
    tiles, tbuf, table, spectra, nexttab, tilesem, xsem, wsem, tsem, nextsem = refs
    shots_here, blocks_here, block_len, tile_len = wbuf.shape
    me_shot, me_freq = lax.axis_index("shot"), lax.axis_index("freq")
    rows = t_ref.shape[2] if load else t_ref.shape[1] // (2 * freq_count)
    groups = [g for chunk in chunks for g in chunk]
    place, stride, start = {}, {}, 0
    for chunk in chunks:
        for j, g in enumerate(chunk):
            place[g], stride[g] = start + j * rows, len(chunk) * rows
        start += len(chunk) * freq_count * rows

    def x_copy(i):
        return pltpu.make_async_copy(x_hbm.at[i], xbuf.at[i], xsem.at[i])

    def w_copy(i):
        return pltpu.make_async_copy(w_hbm.at[i, pl.ds(me_freq * blocks_here, blocks_here)], wbuf.at[i], wsem.at[i])

    def t_copy(i):
        return pltpu.make_async_copy(t_ref.at[:, jnp.bitwise_xor(me_freq, i)], tbuf.at[:, i], tsem.at[i])

    def next_copy(i):
        return pltpu.make_async_copy(next_hbm.at[:, jnp.bitwise_xor(me_freq, i)], nexttab.at[:, i], nextsem.at[i])

    def prepare(source, target):
        for n in range(source.shape[0]):
            high, low = split(jnp.concatenate([source[n, i] for i in range(freq_count)], axis=0))
            target[n] = jnp.concatenate([high, low], axis=0)

    tile_copy = pltpu.make_async_copy(tiles_hbm, tiles, tilesem)
    tile_copy.start()
    if load:
        for i in range(freq_count):
            t_copy(i).start()
        x_copy(0).start()
        w_copy(0).start()
        for i in range(1, DEPTH):
            x_copy(i).start()
    for out in outs:
        out[...] = jnp.zeros_like(out)
    if load:
        for i in range(freq_count):
            t_copy(i).wait()
    if load:
        prepare(tbuf, table)
    else:
        table = t_ref

    def transform(i, n, part):
        high, low = split(part)
        wide = dot_nt(table[n], high)
        half = wide.shape[0] // 2
        result = wide[:half] + wide[half:] + dot_nt(table[n, :half], low)
        g = groups[n]
        for j in range(freq_count):
            start = place[g] + j * stride[g]
            spectra[i % 2, start : start + rows] = result[j * rows : (j + 1) * rows]

    def spread(i, b):
        if load and b == 0:
            w_copy(i).wait()
        if i == 0 and b == 0:
            tile_copy.wait()
        s_high, s_low = split(spectra[i % 2, :, b * block_len : (b + 1) * block_len])
        w_high, w_low = split(wbuf[i, b])
        weights = jnp.concatenate(
            [
                jnp.concatenate([w_high, w_low], axis=1),
                jnp.concatenate([w_high, jnp.zeros_like(w_low)], axis=1),
            ],
            axis=0,
        )
        both = jnp.dot(jnp.concatenate([s_high, s_low], axis=1), weights, preferred_element_type=jnp.float32)
        value = both[:, :tile_len] + both[:, tile_len:]
        tile = tiles[i, me_freq * blocks_here + b]
        start = 0
        for out, orders in zip(outs, steps):
            for slot in slots_of(tile, me_shot, orders, freq_count):
                out[slot] += value[start : start + out.shape[1]]
                start += out.shape[1]

    for i in range(shots_here + 1):
        folded = ()
        if i < shots_here:
            if load:
                x_copy(i).wait()
                if i + DEPTH < shots_here:
                    x_copy(i + DEPTH).start()
                if i == 0:
                    for j in range(freq_count):
                        next_copy(j).start()
                if i == shots_here // 2:
                    for j in range(freq_count):
                        next_copy(j).wait()
                    prepare(nexttab, nextbuf)
                if i + 1 < shots_here:
                    w_copy(i + 1).start()
            folded = fold(xbuf[i], groups)
        for k in range(max(len(folded), blocks_here)):
            if k < len(folded):
                transform(i, k, folded[k])
            if i and k < blocks_here:
                spread(i - 1, k)

def bin_blocks(tile_ids, traces, interp_weights, tables, chunks, steps, shot_count, freq_count, following):
    load = following is not None
    shots_here, recs_here, time_len = traces.shape
    block_len, tile_len = interp_weights.shape[2:]
    blocks_here = recs_here // block_len
    groups = [g for chunk in chunks for g in chunk]
    rows = freq_count * tables.shape[2] if load else tables.shape[1] // 2
    slot_count = shot_count * freq_count * TILES_DEV
    kept = [
        jax.ShapeDtypeStruct(traces.shape, jnp.float32),
        jax.ShapeDtypeStruct((shots_here, blocks_here, block_len, tile_len), jnp.float32),
    ]
    total = slot_count * len(GROUPS) * rows // freq_count * tile_len * 4
    sums = pltpu.VMEM if total <= VMEM_SUMS else jax.ShapeDtypeStruct
    out_shape = [sums((slot_count, rows // freq_count * len(chunk), tile_len), jnp.float32) for chunk in chunks]
    scratch = [
        pltpu.SMEM(tile_ids.shape, jnp.int32),
        pltpu.VMEM(tables.shape, jnp.float32),
        pltpu.VMEM((len(groups), 2 * rows, tables.shape[-1]), jnp.bfloat16),
        pltpu.VMEM((2, len(groups) * rows, recs_here), jnp.float32),
        pltpu.VMEM(tables.shape if following is None else following.shape, jnp.float32),
        pltpu.SemaphoreType.DMA,
        pltpu.SemaphoreType.DMA((shots_here,)),
        pltpu.SemaphoreType.DMA((shots_here,)),
        pltpu.SemaphoreType.DMA((freq_count,)),
        pltpu.SemaphoreType.DMA((freq_count,)),
    ]
    if load:
        count, _, part, depth = following.shape
        kept.append(jax.ShapeDtypeStruct((count, 2 * freq_count * part, depth), jnp.bfloat16))
        out_shape += [pltpu.VMEM(k.shape, k.dtype) for k in kept]
    place = pltpu.HBM if load else pltpu.VMEM

    def body(*refs):
        bin_kernel(chunks, steps, freq_count, load, *refs)

    tile_ids = pltpu.with_memory_space_constraint(tile_ids, pltpu.HBM)
    traces = pltpu.with_memory_space_constraint(traces, place)
    interp_weights = pltpu.with_memory_space_constraint(interp_weights, place)
    tables = pltpu.with_memory_space_constraint(tables, place)
    more = [pltpu.with_memory_space_constraint(following, pltpu.HBM)] if load else []
    return pl.pallas_call(
        body,
        in_specs=[
            pl.BlockSpec(memory_space=pltpu.HBM),
            pl.BlockSpec(memory_space=place),
            pl.BlockSpec(memory_space=place),
            pl.BlockSpec(memory_space=place),
        ]
        + [pl.BlockSpec(memory_space=pltpu.HBM)] * load,
        out_specs=[pl.BlockSpec(memory_space=pltpu.VMEM)] * len(out_shape),
        out_shape=out_shape,
        scratch_shapes=scratch,
        compiler_params=pltpu.CompilerParams(vmem_limit_bytes=VMEM_LIMIT),
        name="bin_blocks",
    )(tile_ids, traces, interp_weights, tables, *more)


def assemble_kernel(*refs):
    out = refs[-1]
    freq_here = out.shape[2]
    for n, chunk in enumerate(CHUNKS):
        rows = refs[2 * n].shape[1] // len(chunk)
        for tile in range(TILES_DEV):
            value = refs[2 * n][tile] + refs[2 * n + 1][tile]
            for j, g in enumerate(chunk):
                stride = 4 if GROUPS[g][0] % 2 == 0 else 8
                residues = GROUPS[g][:1] if stride == 4 else GROUPS[g]
                size = freq_here // stride
                start = j * rows
                for residue in residues:
                    for part in range(2):
                        out[tile, part, pl.ds(residue, size, stride)] = value[start : start + size]
                        start += size


def assemble(last, freq_here, tile_len):
    last = [pltpu.with_memory_space_constraint(value, pltpu.VMEM) for value in last]
    return pl.pallas_call(
        assemble_kernel,
        in_specs=[pl.BlockSpec(memory_space=pltpu.VMEM)] * len(last),
        out_specs=pl.BlockSpec(memory_space=pltpu.VMEM),
        out_shape=jax.ShapeDtypeStruct((TILES_DEV, 2, freq_here, tile_len), jnp.float32),
        name="assemble",
    )(*last)


def shards(traces, interp_weights, tile_ids):
    shot_count = lax.axis_size("shot")
    freq_count = lax.axis_size("freq")
    tile_len = interp_weights.shape[3]
    steps = halvings(shot_count, freq_count)

    def halve(value, ways):
        pairs = []
        for shot in range(shot_count):
            for freq in range(freq_count):
                axis, bit = ways[shot & 1]
                to = (shot ^ (1 << bit), freq) if axis == "shot" else (shot, freq ^ (1 << bit))
                pairs.append((shot * freq_count + freq, to[0] * freq_count + to[1]))
        half = value.shape[0] // 2
        return value[:half], lax.ppermute(value[half:], ("shot", "freq"), pairs)

    sums = [None] * len(CHUNKS)
    first, following = (
        jnp.asarray(dft_tables([g for c in call for g in CHUNKS[c]], freq_count, traces.shape[2])) for call in CALLS
    )
    for n, call in enumerate(CALLS):
        chunks = tuple(CHUNKS[c] for c in call)
        made = bin_blocks(
            tile_ids,
            traces,
            interp_weights,
            following if n else first,
            chunks,
            [steps[c] for c in call],
            shot_count,
            freq_count,
            None if n else following,
        )
        for c, value in zip(call, made):
            sums[c] = value
        if len(made) > len(call):
            traces, interp_weights, following = made[len(call) :]
    last = []
    for orders, value in zip(steps, sums):
        for ways in [(("shot", 0), ("shot", 0)), *zip(*orders)]:
            kept, got = halve(value, ways)
            value = kept + got
        last += [kept, got]
    return assemble(last, NF // freq_count, tile_len)


def solution(mesh):
    in_specs = (P("shot", "freq", None), P("shot", None, None, None), P("shot", None))
    out_specs = P("shot", None, "freq", None)
    return jax.shard_map(shards, mesh=mesh, in_specs=in_specs, out_specs=out_specs, check_vma=False)
```

```python
import math

import jax
import jax.numpy as jnp
import numpy as np
from jax import lax
from jax.experimental import pallas as pl
from jax.experimental.pallas import tpu as pltpu
from jax.sharding import PartitionSpec as P

NF = 384
TILES_DEV = 2
GROUPS = ((0, 4), (2, 6), (1, 7), (3, 5))
CHUNKS = ((0, 1), (2, 3))
ORDERS = (("ayxb", "xaby"), ("yaxb", "xyab"))
CALLS = ((0,), (1,))
DEPTH = 2
VMEM_SUMS = 16 << 20
VMEM_LIMIT = 24 << 20


def halvings(shot_count, freq_count):
    shot_bits = [("shot", bit) for bit in range(1, shot_count.bit_length() - 1)]
    freq_bits = [("freq", bit) for bit in range(freq_count.bit_length() - 1)]
    x, a = len(shot_bits) // 2, len(freq_bits) // 2
    steps = dict(x=shot_bits[:x], y=shot_bits[x:], a=freq_bits[:a], b=freq_bits[a:])
    return [[[step for name in order for step in steps[name]] for order in orders] for orders in ORDERS]


def dft_tables(groups, freq_count, time_len):
    freq_here = NF // freq_count
    scale = 1.0 / math.sqrt(time_len)
    tables = []
    for g in groups:
        residues = GROUPS[g]
        rows = []
        for owner in range(freq_count):
            if residues[0] % 2 == 0:
                freqs = owner * freq_here + np.arange(residues[0], freq_here, 4)
                angle = 2.0 * math.pi / time_len * (freqs[:, None] * np.arange(time_len // 4) % time_len)
                rows += [np.cos(angle), -np.sin(angle)]
            else:
                for residue in residues:
                    freqs = owner * freq_here + np.arange(residue, freq_here, 8)
                    angle = 2.0 * math.pi / time_len * (freqs[:, None] * np.arange(time_len // 8) % time_len)
                    cos, sin = np.cos(angle), np.sin(angle)
                    sign = 1.0 if residue in (1, 5) else -1.0
                    rows += [np.hstack([cos, -sign * sin]), np.hstack([-sin, -sign * cos])]
        tables.append((np.concatenate(rows) * scale).reshape(freq_count, -1, time_len // 4))
    return np.stack(tables).astype(np.float32)


def fold(x, groups):
    eighth = x.shape[1] // 8
    q0, q1, q2, q3 = (x[:, 2 * i * eighth : 2 * (i + 1) * eighth] for i in range(4))
    folded = {}
    if 0 in groups or 1 in groups:
        plus, cross = q0 + q2, q1 + q3
        folded[0], folded[1] = plus + cross, plus - cross
    if 2 in groups or 3 in groups:
        d02, d13 = q0 - q2, q1 - q3
        d0, d1, d2, d3 = d02[:, :eighth], d02[:, eighth:], d13[:, :eighth], d13[:, eighth:]
        root = math.sqrt(0.5)
        near, far = (d1 - d3) * root, (d1 + d3) * root
        folded[2] = jnp.concatenate([d0 + near, d2 + far], axis=1)
        folded[3] = jnp.concatenate([d0 - near, d2 - far], axis=1)
    return [folded[g] for g in groups]


def split(value):
    high = value.astype(jnp.bfloat16)
    return high, (value - high.astype(jnp.float32)).astype(jnp.bfloat16)


def dot_nt(a, b):
    return lax.dot_general(a, b, (((1,), (1,)), ((), ())), preferred_element_type=jnp.float32)


def slots_of(tile, me_shot, steps, freq_count):
    owner = tile // TILES_DEV
    apart = jnp.bitwise_xor(owner, me_shot)
    second = jnp.bitwise_and(owner, 1) == 1
    count = len(steps[0])
    base = jnp.bitwise_and(apart, 1) << count
    for axis, bit in steps[0]:
        if axis == "shot":
            flag = jnp.bitwise_and(jnp.right_shift(apart, bit), 1)
            places = [count - 1 - order.index((axis, bit)) for order in steps]
            base += jnp.where(second, flag << places[1], flag << places[0])
    slots = []
    for far in range(freq_count):
        places = [
            sum((far >> bit & 1) << (count - 1 - i) for i, (axis, bit) in enumerate(order) if axis == "freq")
            for order in steps
        ]
        slots.append((base + jnp.where(second, places[1], places[0])) * TILES_DEV + tile % TILES_DEV)
    return slots


def bin_kernel(chunks, steps, freq_count, load, tiles_hbm, x_ref, w_ref, t_ref, *refs):
    if load:
        next_hbm, refs = refs[0], refs[1:]
    outs, refs = refs[: len(chunks)], refs[len(chunks) :]
    if load:
        x_hbm, w_hbm, xbuf, wbuf, nextbuf = x_ref, w_ref, *refs[:3]
        refs = refs[3:]
    else:
        xbuf, wbuf = x_ref, w_ref
    tiles, tbuf, table, spectra, tilesem, xsem, wsem, tsem, nextsem = refs
    shots_here, blocks_here, block_len, tile_len = wbuf.shape
    me_shot, me_freq = lax.axis_index("shot"), lax.axis_index("freq")
    rows = t_ref.shape[2]
    groups = [g for chunk in chunks for g in chunk]
    place, stride, start = {}, {}, 0
    for chunk in chunks:
        for j, g in enumerate(chunk):
            place[g], stride[g] = start + j * rows, len(chunk) * rows
        start += len(chunk) * freq_count * rows

    def x_copy(i):
        return pltpu.make_async_copy(x_hbm.at[i], xbuf.at[i], xsem.at[i])

    def w_copy(i):
        return pltpu.make_async_copy(w_hbm.at[i, pl.ds(me_freq * blocks_here, blocks_here)], wbuf.at[i], wsem.at[i])

    def t_copy(i):
        return pltpu.make_async_copy(t_ref.at[:, jnp.bitwise_xor(me_freq, i)], tbuf.at[:, i], tsem.at[i])

    def near_table(n, i):
        return tbuf[n, i] if load else t_ref[n, jnp.bitwise_xor(me_freq, i)]

    tile_copy = pltpu.make_async_copy(tiles_hbm, tiles, tilesem)
    tile_copy.start()
    if load:
        for i in range(freq_count):
            t_copy(i).start()
        x_copy(0).start()
        w_copy(0).start()
        for i in range(1, DEPTH):
            x_copy(i).start()
    for out in outs:
        out[...] = jnp.zeros_like(out)
    if load:
        for i in range(freq_count):
            t_copy(i).wait()
    for n in range(len(groups)):
        high, low = split(jnp.concatenate([near_table(n, i) for i in range(freq_count)], axis=0))
        table[n] = jnp.concatenate([high, low], axis=0)

    def transform(i, n, part):
        high, low = split(part)
        wide = dot_nt(table[n], high)
        half = wide.shape[0] // 2
        result = wide[:half] + wide[half:] + dot_nt(table[n, :half], low)
        g = groups[n]
        for j in range(freq_count):
            start = place[g] + j * stride[g]
            spectra[i % 2, start : start + rows] = result[j * rows : (j + 1) * rows]

    def spread(i, b):
        if load and b == 0:
            w_copy(i).wait()
        if i == 0 and b == 0:
            tile_copy.wait()
        s_high, s_low = split(spectra[i % 2, :, b * block_len : (b + 1) * block_len])
        w_high, w_low = split(wbuf[i, b])
        weights = jnp.concatenate(
            [
                jnp.concatenate([w_high, w_low], axis=1),
                jnp.concatenate([w_high, jnp.zeros_like(w_low)], axis=1),
            ],
            axis=0,
        )
        both = jnp.dot(jnp.concatenate([s_high, s_low], axis=1), weights, preferred_element_type=jnp.float32)
        value = both[:, :tile_len] + both[:, tile_len:]
        tile = tiles[i, me_freq * blocks_here + b]
        start = 0
        for out, orders in zip(outs, steps):
            for slot in slots_of(tile, me_shot, orders, freq_count):
                out[slot] += value[start : start + out.shape[1]]
                start += out.shape[1]

    for i in range(shots_here + 1):
        folded = ()
        if i < shots_here:
            if load:
                x_copy(i).wait()
                if i + DEPTH < shots_here:
                    x_copy(i + DEPTH).start()
                if i == shots_here - 1:
                    next_copy = pltpu.make_async_copy(next_hbm, nextbuf, nextsem)
                    next_copy.start()
                if i + 1 < shots_here:
                    w_copy(i + 1).start()
            folded = fold(xbuf[i], groups)
        for k in range(max(len(folded), blocks_here)):
            if k < len(folded):
                transform(i, k, folded[k])
            if i and k < blocks_here:
                spread(i - 1, k)
    if load:
        next_copy.wait()


def bin_blocks(tile_ids, traces, interp_weights, tables, chunks, steps, shot_count, freq_count, following):
    load = following is not None
    shots_here, recs_here, time_len = traces.shape
    block_len, tile_len = interp_weights.shape[2:]
    blocks_here = recs_here // block_len
    groups = [g for chunk in chunks for g in chunk]
    rows = freq_count * tables.shape[2]
    slot_count = shot_count * freq_count * TILES_DEV
    kept = [
        jax.ShapeDtypeStruct(traces.shape, jnp.float32),
        jax.ShapeDtypeStruct((shots_here, blocks_here, block_len, tile_len), jnp.float32),
    ]
    total = slot_count * len(GROUPS) * tables.shape[2] * tile_len * 4
    sums = pltpu.VMEM if total <= VMEM_SUMS else jax.ShapeDtypeStruct
    out_shape = [sums((slot_count, tables.shape[2] * len(chunk), tile_len), jnp.float32) for chunk in chunks]
    scratch = [
        pltpu.SMEM(tile_ids.shape, jnp.int32),
        pltpu.VMEM(tables.shape, jnp.float32),
        pltpu.VMEM((len(groups), 2 * rows, tables.shape[3]), jnp.bfloat16),
        pltpu.VMEM((2, len(groups) * rows, recs_here), jnp.float32),
        pltpu.SemaphoreType.DMA,
        pltpu.SemaphoreType.DMA((shots_here,)),
        pltpu.SemaphoreType.DMA((shots_here,)),
        pltpu.SemaphoreType.DMA((freq_count,)),
        pltpu.SemaphoreType.DMA,
    ]
    if load:
        out_shape += [pltpu.VMEM(k.shape, k.dtype) for k in [*kept, following]]
    place = pltpu.HBM if load else pltpu.VMEM

    def body(*refs):
        bin_kernel(chunks, steps, freq_count, load, *refs)

    tile_ids = pltpu.with_memory_space_constraint(tile_ids, pltpu.HBM)
    traces = pltpu.with_memory_space_constraint(traces, place)
    interp_weights = pltpu.with_memory_space_constraint(interp_weights, place)
    tables = pltpu.with_memory_space_constraint(tables, place)
    more = [pltpu.with_memory_space_constraint(following, pltpu.HBM)] if load else []
    return pl.pallas_call(
        body,
        in_specs=[
            pl.BlockSpec(memory_space=pltpu.HBM),
            pl.BlockSpec(memory_space=place),
            pl.BlockSpec(memory_space=place),
            pl.BlockSpec(memory_space=place),
        ]
        + [pl.BlockSpec(memory_space=pltpu.HBM)] * load,
        out_specs=[pl.BlockSpec(memory_space=pltpu.VMEM)] * len(out_shape),
        out_shape=out_shape,
        scratch_shapes=scratch,
        compiler_params=pltpu.CompilerParams(vmem_limit_bytes=VMEM_LIMIT),
        name="bin_blocks",
    )(tile_ids, traces, interp_weights, tables, *more)


def assemble_kernel(*refs):
    out = refs[-1]
    freq_here = out.shape[2]
    for n, chunk in enumerate(CHUNKS):
        rows = refs[2 * n].shape[1] // len(chunk)
        for tile in range(TILES_DEV):
            value = refs[2 * n][tile] + refs[2 * n + 1][tile]
            for j, g in enumerate(chunk):
                stride = 4 if GROUPS[g][0] % 2 == 0 else 8
                residues = GROUPS[g][:1] if stride == 4 else GROUPS[g]
                size = freq_here // stride
                start = j * rows
                for residue in residues:
                    for part in range(2):
                        out[tile, part, pl.ds(residue, size, stride)] = value[start : start + size]
                        start += size


def assemble(last, freq_here, tile_len):
    last = [pltpu.with_memory_space_constraint(value, pltpu.VMEM) for value in last]
    return pl.pallas_call(
        assemble_kernel,
        in_specs=[pl.BlockSpec(memory_space=pltpu.VMEM)] * len(last),
        out_specs=pl.BlockSpec(memory_space=pltpu.VMEM),
        out_shape=jax.ShapeDtypeStruct((TILES_DEV, 2, freq_here, tile_len), jnp.float32),
        name="assemble",
    )(*last)


def shards(traces, interp_weights, tile_ids):
    shot_count = lax.axis_size("shot")
    freq_count = lax.axis_size("freq")
    tile_len = interp_weights.shape[3]
    steps = halvings(shot_count, freq_count)

    def halve(value, ways):
        pairs = []
        for shot in range(shot_count):
            for freq in range(freq_count):
                axis, bit = ways[shot & 1]
                to = (shot ^ (1 << bit), freq) if axis == "shot" else (shot, freq ^ (1 << bit))
                pairs.append((shot * freq_count + freq, to[0] * freq_count + to[1]))
        half = value.shape[0] // 2
        return value[:half], lax.ppermute(value[half:], ("shot", "freq"), pairs)

    sums = [None] * len(CHUNKS)
    first, following = (
        jnp.asarray(dft_tables([g for c in call for g in CHUNKS[c]], freq_count, traces.shape[2])) for call in CALLS
    )
    for n, call in enumerate(CALLS):
        chunks = tuple(CHUNKS[c] for c in call)
        made = bin_blocks(
            tile_ids,
            traces,
            interp_weights,
            following if n else first,
            chunks,
            [steps[c] for c in call],
            shot_count,
            freq_count,
            None if n else following,
        )
        for c, value in zip(call, made):
            sums[c] = value
        if len(made) > len(call):
            traces, interp_weights, following = made[len(call) :]
    last = []
    for orders, value in zip(steps, sums):
        for ways in [(("shot", 0), ("shot", 0)), *zip(*orders)]:
            kept, got = halve(value, ways)
            value = kept + got
        last += [kept, got]
    return assemble(last, NF // freq_count, tile_len)


def solution(mesh):
    in_specs = (P("shot", "freq", None), P("shot", None, None, None), P("shot", None))
    out_specs = P("shot", None, "freq", None)
    return jax.shard_map(shards, mesh=mesh, in_specs=in_specs, out_specs=out_specs, check_vma=False)
```
